256 devices in a mesh: zslab: 4 (over x_hi, core), angle: 64 (over y, z, x_lo).
Axes of the slice: x: 4 (x_hi: 2, x_lo: 2; x = x_hi * 2 + x_lo), y: 4, z: 8, core: 2. Of those that a mesh axis runs over, the one named last changes fastest.
Arguments:
- measured: float32 [512, 4, 2048], P('angle', 'zslab'), may hold values from -6 to 6
- basis_time: float32 [32, 8], replicated, may hold values from -2.5 to 2.5
- frame_index: int32 [512], P('angle'), may hold values from 0 to 31
- angle_slot: int32 [512], P('angle'), may hold values from 0 to 3
- proj_weights: bfloat16 [256, 128, 256], P('angle'), may hold values from -0.046875 to 0.046875
- tile_offsets: int32 [256, 64, 16], P('angle'), may hold values from 0 to 14
- cone_weights: float32 [3, 512, 4], P(None, 'angle'), may hold values from 0.3 to 1
Outputs:
- coefficients: bfloat16 [64, 8, 4, 2048], P('angle', None, 'zslab')
- misfit: float32 [512, 4, 2048], P('angle', 'zslab')
The draws below stay inside these ranges and needn't reach their ends.
All inputs are finite; a program needn't handle non-finite values.
Results may differ from the reference program's by a relative error of at most 0.0065.
Values may be sent and summed in bfloat16 or wider, within the bound.
A program may use at most 64 MiB of HBM per device.

```python
import jax
import jax.numpy as jnp
from jax import lax

BASIS = 8
WIDTH = 2048
DET = 2048
TILE = 128
FRAMES = 32
ANG_DEV = 4
PROJ_DEV = 8
ROWS = 64
SLICES = 4
ANGLES = 256
PROJS = 512


def touch_ends(drawn, own_key, least, top_value):
    longest = drawn.shape.index(max(drawn.shape))
    spots = []
    for shift in (0, 1):
        where = [jax.random.randint(jax.random.fold_in(own_key, axis), (), 0, length) for axis, length in enumerate(drawn.shape)]
        where[longest] = (where[longest] + shift) % drawn.shape[longest]
        spots.append(tuple(where))
    return drawn.at[spots[0]].set(least).at[spots[1]].set(top_value)


def block_levels(key, dims, split, low, largest):
    level, own = 1.0, jax.random.fold_in(key, 6)
    for dim, shards_of in split:
        steps = jnp.exp(jax.random.uniform(jax.random.fold_in(own, dim), (shards_of,), jnp.float32, low / len(split), largest / len(split)))
        level = level * jnp.repeat(steps, dims[dim] // shards_of).reshape([-1 if axis == dim else 1 for axis in range(len(dims))])
    return level


def scatter_about(key, dims, scale, limit, shards=(), held_as=jnp.bfloat16):
    gain = block_levels(key, dims, shards, -0.22, 0.18) if shards else 1.0
    drawn = jax.random.normal(key, dims, jnp.float32) * scale * gain
    return jnp.minimum(jnp.maximum(drawn, -limit), limit).astype(held_as)


def setup_inputs(seed: int = 0) -> dict:
    seeds = jax.random.split(jax.random.key(seed), 8)
    measured = scatter_about(seeds[0], (PROJS, SLICES, DET), 1.0, 6.0, ((0, 64), (1, 4)), jnp.float32)
    basis_time = scatter_about(seeds[1], (FRAMES, BASIS), 0.35, 2.5, (), jnp.float32)
    frame_index = touch_ends(jax.random.randint(seeds[2], (PROJS,), 0, FRAMES), jax.random.fold_in(seeds[2], 1), 0, FRAMES - 1).astype(jnp.int32)
    angle_slot = touch_ends(jax.random.randint(seeds[3], (PROJS,), 0, ANG_DEV), jax.random.fold_in(seeds[3], 1), 0, ANG_DEV - 1).astype(jnp.int32)
    proj_weights = scatter_about(seeds[4], (ANGLES, TILE, 2 * TILE), (ROWS * 2 * TILE) ** -0.5, 0.046875, ((0, 64),))
    tile_offsets = touch_ends(jax.random.randint(seeds[5], (ANGLES, ROWS, WIDTH // TILE), 0, DET // TILE - 1), jax.random.fold_in(seeds[5], 1), 0, (DET // TILE - 1) - 1).astype(jnp.int32)
    cone_weights = jnp.clip(0.3 + 0.7 * jax.random.uniform(seeds[6], (3, PROJS, SLICES), jnp.float32) ** block_levels(seeds[6], (3, PROJS, SLICES), ((1, 64),), -0.2, 0.2), 0.3, 1.0)
    return {"measured": measured, "basis_time": basis_time, "frame_index": frame_index, "angle_slot": angle_slot, "proj_weights": proj_weights, "tile_offsets": tile_offsets, "cone_weights": cone_weights}


step_scale = 0.4
highest = lax.Precision.HIGHEST


def planar(coeff_fields, proj_weights, tile_offsets):
    pixel_tiles = coeff_fields.astype(jnp.float32).reshape(ROWS, BASIS, SLICES, WIDTH // TILE, TILE)
    pair_steps = jnp.arange(2, dtype=jnp.int32)

    def one_angle(inputs):
        weight_tile, offset_rows = inputs
        response = jnp.einsum("ykziu,ud->kzyid", pixel_tiles, weight_tile.astype(jnp.float32))
        response = response.reshape(BASIS, SLICES, ROWS, WIDTH // TILE, 2, TILE)
        landing = offset_rows[:, :, None] + pair_steps
        blank_planes = jnp.zeros((BASIS, SLICES, DET // TILE, TILE), jnp.float32)
        return blank_planes.at[:, :, landing, :].add(response)

    return lax.map(one_angle, (proj_weights, tile_offsets))


def forward(coeff_fields, proj_weights, tile_offsets, owner_angle, phi_rows, cone_weights):
    planes_all = planar(coeff_fields, proj_weights, tile_offsets)
    chosen = planes_all[owner_angle]
    planes_now = jnp.einsum("pk,pkzjc->pzjc", phi_rows, chosen, precision=highest).reshape(PROJS, SLICES, DET)
    padded = jnp.pad(planes_now, ((0, 0), (1, 1), (0, 0)))
    return (cone_weights[0][:, :, None] * padded[:, :-2] + cone_weights[1][:, :, None] * padded[:, 1:-1]
            + cone_weights[2][:, :, None] * padded[:, 2:])


def gradient(residual, proj_weights, tile_offsets, owner_angle, phi_rows, cone_weights):
    padded = jnp.pad(residual, ((0, 0), (1, 1), (0, 0)))
    cone_pad = jnp.pad(cone_weights, ((0, 0), (0, 0), (1, 1)))
    back_planes = (cone_pad[0][:, 2:, None] * padded[:, 2:] + cone_pad[1][:, 1:-1, None] * padded[:, 1:-1]
                   + cone_pad[2][:, :-2, None] * padded[:, :-2])
    weighted = phi_rows[:, :, None, None] * back_planes[:, None, :, :]
    spread = jax.ops.segment_sum(weighted, owner_angle, num_segments=ANGLES).astype(jnp.bfloat16)
    spread = spread.reshape(ANGLES, BASIS, SLICES, DET // TILE, TILE)
    pair_steps = jnp.arange(2, dtype=jnp.int32)

    def one_angle(running, inputs):
        spread_tile, weight_tile, offset_rows = inputs
        landing = offset_rows[:, :, None] + pair_steps
        picked = spread_tile[:, :, landing, :].astype(jnp.float32)
        contrib = jnp.einsum("kzyihc,uhc->ykziu", picked, weight_tile.astype(jnp.float32).reshape(TILE, 2, TILE))
        return running + contrib.reshape(ROWS, BASIS, SLICES, WIDTH), None

    running, unused = lax.scan(one_angle, jnp.zeros((ROWS, BASIS, SLICES, WIDTH), jnp.float32),
                               (spread, proj_weights, tile_offsets))
    return running


def reference(measured, basis_time, frame_index, angle_slot, proj_weights, tile_offsets, cone_weights):
    owner_angle = (jnp.arange(PROJS, dtype=jnp.int32) // PROJ_DEV) * ANG_DEV + angle_slot
    phi_rows = basis_time[frame_index]
    first_iterate = (step_scale * gradient(measured, proj_weights, tile_offsets, owner_angle, phi_rows,
                                           cone_weights)).astype(jnp.bfloat16)
    misfit = forward(first_iterate, proj_weights, tile_offsets, owner_angle, phi_rows, cone_weights) - measured
    update = gradient(misfit, proj_weights, tile_offsets, owner_angle, phi_rows, cone_weights)
    coefficients = (first_iterate.astype(jnp.float32) - step_scale * update).astype(jnp.bfloat16)
    return coefficients, misfit
```

```python
import functools

import jax
import jax.numpy as jnp
from jax import lax
from jax.experimental import pallas as pl
from jax.experimental.pallas import tpu as pltpu
from jax.sharding import PartitionSpec as P

GRIDS = {64: (4, 8, 2), 8: (2, 2, 2)}
MESH = pl.DeviceIdType.MESH
STEP = 0.4
TILE = 128
BASIS = 8
PROJ = 8
ANG = 4
TILES = 16
SPLIT_PHI = True
f32, bf16, i32 = jnp.float32, jnp.bfloat16, jnp.int32
SLAB_OFFS = (-2, 2, -1, 1)

NN = (((1,), (0,)), ((), ()))
NT = (((1,), (1,)), ((), ()))


def mm(a, b, dims=NN):
    return lax.dot_general(a, b, dims, preferred_element_type=f32)


def split(value):
    high = value.astype(bf16)
    return high, (value - high.astype(f32)).astype(bf16)


def iota(shape, dim):
    return lax.broadcasted_iota(i32, shape, dim)


def kernel(
    grid, slabs,
    meas_ref, basis_ref, frame_ref, slot_ref, w_ref, off_ref, cone_ref,
    coef_ref, misfit_ref,
    meta_send, meta_recv, x_ref, m_ref, ml_ref, halo_ref, plane_ref, planes_ref,
    r1_ref, r2_ref, p1_send, p1_recv, p2_send, p2_recv, first_ref, s_send, s_recv,
    a_ss, a_rs, b_ss, b_rs, z_ss, z_rs,
):
    ny, nz, nx = grid
    na, nb = nz, ny * nx
    slab = lax.axis_index("zslab")
    place = lax.axis_index("angle")
    my_x = place % nx
    alpha = (place // nx) % nz
    my_y = place // (nx * nz)
    beta = my_y * nx + my_x

    a_steps = sorted(range(1, na), key=lambda d: -min(d, na - d))
    b_steps = sorted(
        [(dy, dx) for dy in range(ny) for dx in range(nx) if dy or dx],
        key=lambda s: -(min(s[0], ny - s[0]) + s[1]),
    )

    def a_at(step):
        return lax.rem(alpha + step + na, na)

    def a_device(step):
        return my_y * (nz * nx) + a_at(step) * nx + my_x

    def b_at(step):
        return lax.rem(my_y + step[0] + ny, ny) * nx + lax.rem(my_x + step[1] + nx, nx)

    def b_device(step):
        other = b_at(step)
        return (other // nx) * (nz * nx) + alpha * nx + other % nx

    def a_copy(phase, n, src, dst):
        return pltpu.make_async_remote_copy(
            src_ref=src, dst_ref=dst, send_sem=a_ss.at[phase, n], recv_sem=a_rs.at[phase, n],
            device_id={"angle": a_device(a_steps[n])}, device_id_type=MESH,
        )

    def b_copy(phase, n, src, dst):
        return pltpu.make_async_remote_copy(
            src_ref=src, dst_ref=dst, send_sem=b_ss.at[phase, n], recv_sem=b_rs.at[phase, n],
            device_id={"angle": b_device(b_steps[n])}, device_id_type=MESH,
        )

    def z_valid(step):
        return jnp.logical_and(slab + step >= 0, slab + step < slabs)

    def z_index(step):
        return SLAB_OFFS.index(step)

    def z_copy(phase, step, src, dst_of):
        back_slot = z_index(-step)
        return pltpu.make_async_remote_copy(
            src_ref=src, dst_ref=dst_of(back_slot), send_sem=z_ss.at[phase, z_index(step)],
            recv_sem=z_rs.at[phase, back_slot],
            device_id={"zslab": slab + step}, device_id_type=MESH,
        )

    def z_arrival(phase, step, src, dst_of):
        slot = z_index(step)
        return pltpu.make_async_remote_copy(
            src_ref=src, dst_ref=dst_of(slot), send_sem=z_ss.at[phase, slot],
            recv_sem=z_rs.at[phase, slot],
            device_id={"zslab": slab + step}, device_id_type=MESH,
        )

    barrier = pltpu.get_barrier_semaphore()
    for step in a_steps:
        pl.semaphore_signal(barrier, inc=1, device_id={"angle": a_device(step)}, device_id_type=MESH)
    for step in b_steps:
        pl.semaphore_signal(barrier, inc=1, device_id={"angle": b_device(step)}, device_id_type=MESH)
    for step in range(1, slabs):
        pl.semaphore_signal(
            barrier, inc=1, device_id={"zslab": lax.rem(slab + step, slabs)}, device_id_type=MESH
        )

    slots = [slot_ref[p] for p in range(PROJ)]
    rows = iota((PROJ * TILES, ANG * TILES), 0)
    cols = iota((PROJ * TILES, ANG * TILES), 1)
    slot_rows = jnp.concatenate(
        [jnp.full((TILES, ANG * TILES), slots[p], i32) for p in range(PROJ)], axis=0
    )
    pick = jnp.logical_and((rows & (TILES - 1)) == (cols & (TILES - 1)), slot_rows == (cols >> 4))
    offs = off_ref[...].reshape(ANG * TILES, na * nb).astype(f32).astype(bf16)
    offs_p = mm(pick.astype(f32).astype(bf16), offs)
    order = iota((na * nb, na * nb), 0)
    o_alpha, o_beta = order // nb, order % nb
    image_row = (o_beta // nx) * (nz * nx) + o_alpha * nx + o_beta % nx
    permute = (image_row == iota((na * nb, na * nb), 1)).astype(f32).astype(bf16)
    offs_sent = mm(permute, offs_p.astype(bf16), NT)

    lane_p = iota((32, TILE), 1) >> 4
    frames = jnp.zeros((32, TILE), i32)
    for p in range(PROJ):
        frames = jnp.where(lane_p == p, frame_ref[p], frames)
    hot = (frames == iota((32, TILE), 0)).astype(f32)
    phi = lax.dot_general(
        basis_ref[...], hot, NN, precision=lax.Precision.HIGHEST, preferred_element_type=f32
    )
    for a in range(na):
        meta_send[a, 0:nb, :] = offs_sent[a * nb:(a + 1) * nb]
        meta_send[a, 8:16, :] = phi
    meta_recv[alpha] = meta_send[alpha]

    for step in (-2, 2, -1, 1):
        @pl.when(jnp.logical_not(z_valid(step)))
        def _():
            planes_ref[z_index(step)] = jnp.zeros((TILE, TILE), bf16)
            if abs(step) == 1:
                halo_ref[z_index(step) - 2] = jnp.zeros((TILE, TILE), f32)

    pl.semaphore_wait(barrier, len(a_steps) + len(b_steps) + slabs - 1)

    halo_at = lambda slot: halo_ref.at[slot - 2]
    planes_at = lambda slot: planes_ref.at[slot]
    for step in (-1, 1):
        @pl.when(z_valid(step))
        def _():
            z_copy(0, step, meas_ref, halo_at).start()
    for n, step in enumerate(a_steps):
        a_copy(0, n, meta_send.at[a_at(step)], meta_recv.at[alpha]).start()

    def cone(kind, step, p):
        at = jnp.clip(slab + step, 0, slabs - 1)
        return cone_ref[kind, at, p]

    def cone_masked(kind, step, p):
        return jnp.where(z_valid(step), cone(kind, step, p), 0.0)

    def part(value, p):
        return value[p * TILES:(p + 1) * TILES]

    def back_of(below, here, above):
        return jnp.concatenate([
            cone_masked(0, 1, p) * part(above, p) + cone(1, 0, p) * part(here, p)
            + cone_masked(2, -1, p) * part(below, p)
            for p in range(PROJ)
        ], axis=0)

    def shift_up(value):
        return jnp.concatenate([value[1:], value[:1]], axis=0)

    def shift_down(value):
        return jnp.concatenate([value[-1:], value[:-1]], axis=0)

    def responses(back):
        window = jnp.concatenate([back, shift_up(back)], axis=1)
        high, low = split(window)
        weights = w_ref[...].reshape(ANG * TILE, 2 * TILE)
        every = mm(high, weights, NT) + mm(low, weights, NT)
        picked = []
        for p in range(PROJ):
            block = part(every, p)
            own = jnp.zeros((TILES, TILE), f32)
            for a in range(ANG):
                own = jnp.where(slots[p] == a, block[:, a * TILE:(a + 1) * TILE], own)
            picked.append(own)
        return jnp.concatenate(picked, axis=0)

    def send_responses(phase, r_ref, back):
        r_ref[alpha] = responses(back).astype(bf16)
        for n in range(na - 1):
            a_copy(phase, n, r_ref.at[alpha], r_ref.at[alpha]).start()

    def a_wait(phase, ref_of):
        for n, step in enumerate(a_steps):
            ref = ref_of(n, a_at(-step))
            a_copy(phase, n, ref, ref).wait_recv()

    def b_wait(phase, ref_of):
        for n, step in enumerate(b_steps):
            ref = ref_of(n, b_at((-step[0], -step[1])))
            b_copy(phase, n, ref, ref).wait_recv()

    for step in (-1, 1):
        @pl.when(z_valid(step))
        def _():
            z_arrival(0, step, meas_ref, halo_at).wait_recv()
    measured = meas_ref[...]
    below, above = halo_ref[0], halo_ref[1]
    send_responses(1, r1_ref, back_of(below, measured, above))

    a_wait(0, lambda n, at: meta_recv.at[at])
    near = jnp.concatenate([meta_recv[a, 0:nb, :] for a in range(na)], axis=0).astype(bf16)
    e_row, e_col = iota((TILE, TILE), 0), iota((TILE, TILE), 1)
    same = (e_row >> 4) == (e_col >> 4)
    for i in range(TILES):
        expand = jnp.logical_and(same, (e_row & (TILES - 1)) == i).astype(f32).astype(bf16)
        x_ref[i] = mm(near, expand)
    tile_lane = (iota((BASIS, TILE), 1) & (TILES - 1)).astype(f32)
    phi_high, phi_low = [], []
    for a in range(na):
        value = meta_recv[a, 8:16, :]
        high = value.astype(bf16).astype(f32)
        phi_high.append(high)
        phi_low.append(value - high)

    def build(b, carry):
        for pair in range(TILES // 2):
            for a in range(na):
                high, low = [], []
                for i in (2 * pair, 2 * pair + 1):
                    line = x_ref[i, pl.ds(a * nb + b, 1), :]
                    hit = jnp.broadcast_to(line, (BASIS, TILE)) == tile_lane
                    high.append(jnp.where(hit, phi_high[a], 0.0))
                    low.append(jnp.where(hit, phi_low[a], 0.0))
                at = pl.ds(pl.multiple_of(b * TILE + pair * 16, 16), 16)
                m_ref[at, a * TILE:(a + 1) * TILE] = jnp.concatenate(high, axis=0).astype(bf16)
                if SPLIT_PHI:
                    ml_ref[at, a * TILE:(a + 1) * TILE] = jnp.concatenate(low, axis=0).astype(bf16)
        return carry

    lax.fori_loop(0, nb, build, 0)

    def scatter_gradient(phase, r_ref, p_send, p_recv):
        gathered = r_ref[...].reshape(na * TILE, TILE)

        def rows_of(b):
            at = pl.ds(pl.multiple_of(b * TILE, TILE), TILE)
            value = mm(m_ref[at, :], gathered)
            if SPLIT_PHI:
                value = value + mm(ml_ref[at, :], gathered)
            return value

        for n, step in enumerate(b_steps):
            p_send[n] = rows_of(b_at(step)).astype(bf16)
            b_copy(phase, n, p_send.at[n], p_recv.at[n]).start()
        total = rows_of(beta)
        b_wait(phase, lambda n, at: p_recv.at[n])
        for n in range(nb - 1):
            total = total + p_recv[n].astype(f32)
        return total

    a_wait(1, lambda n, at: r1_ref.at[at])
    first = (STEP * scatter_gradient(0, r1_ref, p1_send, p1_recv)).astype(bf16)
    first32 = first.astype(f32)

    first_ref[beta] = first32.T.astype(bf16)
    for n in range(nb - 1):
        b_copy(1, n, first_ref.at[beta], first_ref.at[beta]).start()
    b_wait(1, lambda n, at: first_ref.at[at])
    fields = jnp.concatenate([first_ref[b] for b in range(nb)], axis=1)

    def sums_of(a):
        at = pl.ds(pl.multiple_of(a * TILE, TILE), TILE)
        value = mm(fields, m_ref[:, at])
        if SPLIT_PHI:
            value = value + mm(fields, ml_ref[:, at])
        return value

    for n, step in enumerate(a_steps):
        s_send[n] = sums_of(a_at(step)).astype(bf16)
        a_copy(2, n, s_send.at[n], s_recv.at[n]).start()
    sums = sums_of(alpha)
    a_wait(2, lambda n, at: s_recv.at[n])
    for n in range(na - 1):
        sums = sums + s_recv[n].astype(f32)
    sums = sums.T
    zero = jnp.zeros((TILES, TILE), f32)
    masked = jnp.concatenate([
        jnp.concatenate([jnp.where(slots[p] == a, part(sums, p), zero) for a in range(ANG)], axis=1)
        for p in range(PROJ)
    ], axis=0)
    high, low = split(masked)
    weights = w_ref[...].reshape(ANG * TILE, 2 * TILE)
    landed = mm(high, weights) + mm(low, weights)
    plane = landed[:, :TILE] + shift_down(landed[:, TILE:])
    plane_ref[...] = plane.astype(bf16)
    for step in SLAB_OFFS:
        @pl.when(z_valid(step))
        def _():
            z_copy(1, step, plane_ref, planes_at).start()
    for step in SLAB_OFFS:
        @pl.when(z_valid(step))
        def _():
            z_arrival(1, step, plane_ref, planes_at).wait_recv()
    planes = {step: planes_ref[z_index(step)].astype(f32) for step in SLAB_OFFS}
    planes[0] = plane
    seen = {-1: below, 0: measured, 1: above}

    def misfit_at(v):
        return jnp.concatenate([
            cone(0, v, p) * part(planes[v - 1], p) + cone(1, v, p) * part(planes[v], p)
            + cone(2, v, p) * part(planes[v + 1], p) - part(seen[v], p)
            for p in range(PROJ)
        ], axis=0)

    misfit = misfit_at(0)
    misfit_ref[...] = misfit

    send_responses(3, r2_ref, back_of(misfit_at(-1), misfit, misfit_at(1)))
    a_wait(3, lambda n, at: r2_ref.at[at])
    update = scatter_gradient(2, r2_ref, p2_send, p2_recv)
    coefficients = (first32 - STEP * update).astype(bf16)
    coef_ref[...] = jnp.concatenate(
        [coefficients[i * BASIS:(i + 1) * BASIS] for i in range(TILES)], axis=1
    )

    for n in range(na - 1):
        a_copy(0, n, meta_send.at[0], meta_recv.at[0]).wait_send()
        a_copy(1, n, r1_ref.at[0], r1_ref.at[0]).wait_send()
        a_copy(2, n, s_send.at[n], s_recv.at[n]).wait_send()
        a_copy(3, n, r2_ref.at[0], r2_ref.at[0]).wait_send()
    for n in range(nb - 1):
        b_copy(0, n, p1_send.at[n], p1_recv.at[n]).wait_send()
        b_copy(1, n, first_ref.at[0], first_ref.at[0]).wait_send()
        b_copy(2, n, p2_send.at[n], p2_recv.at[n]).wait_send()
    for step in SLAB_OFFS:
        @pl.when(z_valid(step))
        def _():
            if abs(step) == 1:
                z_copy(0, step, meas_ref, halo_at).wait_send()
            z_copy(1, step, plane_ref, planes_at).wait_send()


def local(grid, slabs, measured, basis_time, frame_index, angle_slot, proj_weights, tile_offsets, cone_weights):
    ny, nz, nx = grid
    na, nb = nz, ny * nx
    block = (TILE, TILE)
    vmem = pl.BlockSpec(memory_space=pltpu.VMEM)
    smem = pl.BlockSpec(memory_space=pltpu.SMEM)
    coefficients, misfit = pl.pallas_call(
        functools.partial(kernel, grid, slabs),
        out_shape=(
            jax.ShapeDtypeStruct((BASIS, TILES * TILE), bf16),
            jax.ShapeDtypeStruct(block, f32),
        ),
        in_specs=[vmem, vmem, smem, smem, vmem, vmem, smem],
        out_specs=(vmem, vmem),
        scratch_shapes=[
            pltpu.VMEM((na, 16, TILE), f32),
            pltpu.VMEM((na, 16, TILE), f32),
            pltpu.VMEM((TILES, na * nb, TILE), f32),
            pltpu.VMEM((nb * TILE, na * TILE), bf16),
            pltpu.VMEM((nb * TILE, na * TILE), bf16),
            pltpu.VMEM((2,) + block, f32),
            pltpu.VMEM(block, bf16),
            pltpu.VMEM((4,) + block, bf16),
            pltpu.VMEM((na,) + block, bf16),
            pltpu.VMEM((na,) + block, bf16),
            pltpu.VMEM((nb - 1,) + block, bf16),
            pltpu.VMEM((nb - 1,) + block, bf16),
            pltpu.VMEM((nb - 1,) + block, bf16),
            pltpu.VMEM((nb - 1,) + block, bf16),
            pltpu.VMEM((nb,) + block, bf16),
            pltpu.VMEM((na - 1,) + block, bf16),
            pltpu.VMEM((na - 1,) + block, bf16),
            pltpu.SemaphoreType.DMA((4, na - 1)),
            pltpu.SemaphoreType.DMA((4, na - 1)),
            pltpu.SemaphoreType.DMA((3, nb - 1)),
            pltpu.SemaphoreType.DMA((3, nb - 1)),
            pltpu.SemaphoreType.DMA((2, 4)),
            pltpu.SemaphoreType.DMA((2, 4)),
        ],
        compiler_params=pltpu.CompilerParams(
            collective_id=0, has_side_effects=True, vmem_limit_bytes=40 * 1024 * 1024
        ),
        name="two_gradients",
    )(
        measured.reshape(block),
        basis_time.T,
        frame_index,
        angle_slot,
        proj_weights,
        tile_offsets.transpose(0, 2, 1),
        cone_weights.transpose(0, 2, 1),
    )
    return (
        coefficients.reshape(1, BASIS, 1, TILES * TILE),
        misfit.reshape(PROJ, 1, TILES * TILE),
    )


def solution(mesh):
    placed = (
        P("angle", "zslab", None),
        P(),
        P("angle"),
        P("angle"),
        P("angle", None, None),
        P("angle", None, None),
        P(None, "angle", None),
    )
    grid = GRIDS[mesh.shape["angle"]]
    return jax.shard_map(
        functools.partial(local, grid, mesh.shape["zslab"]),
        mesh=mesh,
        in_specs=placed,
        out_specs=(P("angle", None, "zslab", None), P("angle", "zslab", None)),
        check_vma=False,
    )
```

```python
import functools

import jax
import jax.numpy as jnp
from jax import lax
from jax.experimental import pallas as pl
from jax.experimental.pallas import tpu as pltpu
from jax.sharding import PartitionSpec as P

GRIDS = {64: (4, 8, 2), 8: (2, 2, 2)}
MESH = pl.DeviceIdType.MESH
STEP = 0.4
TILE = 128
BASIS = 8
PROJ = 8
ANG = 4
TILES = 16
SPLIT_PHI = False
CHUNKS = 2
UC = TILE // CHUNKS
f32, bf16, i32 = jnp.float32, jnp.bfloat16, jnp.int32
SLAB_OFFS = (-2, 2, -1, 1)

NN = (((1,), (0,)), ((), ()))
NT = (((1,), (1,)), ((), ()))


def mm(a, b, dims=NN):
    return lax.dot_general(a, b, dims, preferred_element_type=f32)


def split(value):
    high = value.astype(bf16)
    return high, (value - high.astype(f32)).astype(bf16)


def iota(shape, dim):
    return lax.broadcasted_iota(i32, shape, dim)


def kernel(
    grid, slabs,
    meas_hbm, basis_hbm, frame_hbm, slot_hbm, w_hbm, off_hbm, cone_hbm,
    coef_ref, misfit_ref,
    meas_ref, basis_ref, frame_ref, slot_ref, w_ref, off_ref, cone_ref, load_sem,
    meta_send, meta_recv, x_ref, m_ref, ml_ref, near_ref, edge_ref, far_ref, plane_ref, planes_ref,
    r1_ref, r2_ref, p1_send, p1_recv, p2_send, p2_recv, first_ref, s_send, s_recv,
    a_ss, a_rs, b_ss, b_rs, z_ss, z_rs, h_ss, h_rs,
):
    ny, nz, nx = grid
    na, nb = nz, ny * nx
    slab = lax.axis_index("zslab")
    place = lax.axis_index("angle")
    my_x = place % nx
    alpha = (place // nx) % nz
    my_y = place // (nx * nz)
    beta = my_y * nx + my_x

    a_steps = sorted(range(1, na), key=lambda d: -min(d, na - d))
    b_steps = sorted(
        [(dy, dx) for dy in range(ny) for dx in range(nx) if dy or dx],
        key=lambda s: -(min(s[0], ny - s[0]) + s[1]),
    )

    def a_at(step):
        return lax.rem(alpha + step + na, na)

    def a_device(step):
        return my_y * (nz * nx) + a_at(step) * nx + my_x

    def b_at(step):
        return lax.rem(my_y + step[0] + ny, ny) * nx + lax.rem(my_x + step[1] + nx, nx)

    def b_device(step):
        other = b_at(step)
        return (other // nx) * (nz * nx) + alpha * nx + other % nx

    def a_copy(phase, c, n, src, dst):
        return pltpu.make_async_remote_copy(
            src_ref=src, dst_ref=dst, send_sem=a_ss.at[phase, c, n], recv_sem=a_rs.at[phase, c, n],
            device_id={"angle": a_device(a_steps[n])}, device_id_type=MESH,
        )

    def b_copy(phase, c, n, src, dst):
        return pltpu.make_async_remote_copy(
            src_ref=src, dst_ref=dst, send_sem=b_ss.at[phase, c, n], recv_sem=b_rs.at[phase, c, n],
            device_id={"angle": b_device(b_steps[n])}, device_id_type=MESH,
        )

    def z_valid(step):
        return jnp.logical_and(slab + step >= 0, slab + step < slabs)

    def z_index(step):
        return SLAB_OFFS.index(step)

    def z_copy(step):
        back_slot = z_index(-step)
        return pltpu.make_async_remote_copy(
            src_ref=plane_ref, dst_ref=planes_ref.at[back_slot], send_sem=z_ss.at[z_index(step)],
            recv_sem=z_rs.at[back_slot], device_id={"zslab": slab + step}, device_id_type=MESH,
        )

    def z_arrival(step):
        slot = z_index(step)
        return pltpu.make_async_remote_copy(
            src_ref=plane_ref, dst_ref=planes_ref.at[slot], send_sem=z_ss.at[slot],
            recv_sem=z_rs.at[slot], device_id={"zslab": slab + step}, device_id_type=MESH,
        )

    odd = slab % 2
    near_copy = pltpu.make_async_remote_copy(
        src_ref=meas_ref, dst_ref=near_ref, send_sem=h_ss.at[0], recv_sem=h_rs.at[0],
        device_id={"zslab": slab + 1 - 2 * odd}, device_id_type=MESH,
    )
    far_step = 2 * odd - 1
    far_valid = jnp.logical_and(slab + far_step >= 0, slab + far_step < slabs)
    far_copy = pltpu.make_async_remote_copy(
        src_ref=edge_ref, dst_ref=far_ref, send_sem=h_ss.at[1], recv_sem=h_rs.at[1],
        device_id={"zslab": slab + far_step}, device_id_type=MESH,
    )

    loads = [
        pltpu.make_async_copy(source, target, load_sem.at[n])
        for n, (source, target) in enumerate([
            (slot_hbm, slot_ref), (off_hbm, off_ref), (frame_hbm, frame_ref), (basis_hbm, basis_ref),
            (meas_hbm, meas_ref), (cone_hbm, cone_ref), (w_hbm, w_ref),
        ])
    ]
    for load in loads:
        load.start()

    sent = []

    def send(copy, valid=None):
        if valid is None:
            copy.start()
        else:
            pl.when(valid)(copy.start)
        sent.append((copy, valid))

    def finish():
        for copy, valid in sent:
            if valid is None:
                copy.wait_send()
            else:
                pl.when(valid)(copy.wait_send)

    barrier = pltpu.get_barrier_semaphore()
    for step in a_steps:
        pl.semaphore_signal(barrier, inc=1, device_id={"angle": a_device(step)}, device_id_type=MESH)
    for step in b_steps:
        pl.semaphore_signal(barrier, inc=1, device_id={"angle": b_device(step)}, device_id_type=MESH)
    for step in range(1, slabs):
        pl.semaphore_signal(
            barrier, inc=1, device_id={"zslab": lax.rem(slab + step, slabs)}, device_id_type=MESH
        )

    for load in loads[:4]:
        load.wait()
    slots = [slot_ref[p] for p in range(PROJ)]
    rows = iota((PROJ * TILES, ANG * TILES), 0)
    cols = iota((PROJ * TILES, ANG * TILES), 1)
    slot_rows = jnp.concatenate(
        [jnp.full((TILES, ANG * TILES), slots[p], i32) for p in range(PROJ)], axis=0
    )
    pick = jnp.logical_and((rows & (TILES - 1)) == (cols & (TILES - 1)), slot_rows == (cols >> 4))
    offs = off_ref[...].reshape(ANG * TILES, na * nb).astype(f32).astype(bf16)
    offs_p = mm(pick.astype(f32).astype(bf16), offs)
    order = iota((na * nb, na * nb), 0)
    o_alpha, o_beta = order // nb, order % nb
    image_row = (o_beta // nx) * (nz * nx) + o_alpha * nx + o_beta % nx
    permute = (image_row == iota((na * nb, na * nb), 1)).astype(f32).astype(bf16)
    offs_sent = mm(permute, offs_p.astype(bf16), NT)

    lane_p = iota((32, TILE), 1) >> 4
    frames = jnp.zeros((32, TILE), i32)
    for p in range(PROJ):
        frames = jnp.where(lane_p == p, frame_ref[p], frames)
    hot = (frames == iota((32, TILE), 0)).astype(f32)
    phi = lax.dot_general(
        basis_ref[...], hot, NN, precision=lax.Precision.HIGHEST, preferred_element_type=f32
    )
    for a in range(na):
        meta_send[a, 0:nb, :] = offs_sent[a * nb:(a + 1) * nb]
        meta_send[a, 8:16, :] = phi
    meta_recv[alpha] = meta_send[alpha]

    for step in SLAB_OFFS:
        @pl.when(jnp.logical_not(z_valid(step)))
        def _():
            planes_ref[z_index(step)] = jnp.zeros((TILE, TILE), bf16)

    @pl.when(jnp.logical_not(far_valid))
    def _():
        far_ref[...] = jnp.zeros((TILE, TILE), bf16)

    for load in loads[4:]:
        load.wait()
    edge_ref[...] = meas_ref[...].astype(bf16)
    pl.semaphore_wait(barrier, len(a_steps) + len(b_steps) + slabs - 1)

    send(far_copy, far_valid)
    send(near_copy)
    for n, step in enumerate(a_steps):
        send(a_copy(0, 0, n, meta_send.at[a_at(step)], meta_recv.at[alpha]))

    def cone(kind, step, p):
        at = jnp.clip(slab + step, 0, slabs - 1)
        return cone_ref[kind, at, p]

    def cone_masked(kind, step, p):
        return jnp.where(z_valid(step), cone(kind, step, p), 0.0)

    def part(value, p):
        return value[p * TILES:(p + 1) * TILES]

    def back_of(below, here, above):
        return jnp.concatenate([
            cone_masked(0, 1, p) * part(above, p) + cone(1, 0, p) * part(here, p)
            + cone_masked(2, -1, p) * part(below, p)
            for p in range(PROJ)
        ], axis=0)

    def shift_up(value):
        return jnp.concatenate([value[1:], value[:1]], axis=0)

    def shift_down(value):
        return jnp.concatenate([value[-1:], value[:-1]], axis=0)

    weights = w_ref[...].reshape(ANG * TILE, 2 * TILE)
    slot_lane = jnp.concatenate(
        [jnp.full((8, TILES), slots[p], i32) for p in range(PROJ)], axis=1
    )

    def send_responses(phase, r_ref, back):
        high, low = split(jnp.concatenate([back, shift_up(back)], axis=1))
        every = mm(weights, high, NT) + mm(weights, low, NT)
        owner = jnp.broadcast_to(slot_lane[:1], (UC, TILE))
        for c in range(CHUNKS):
            own = jnp.zeros((UC, TILE), f32)
            for a in range(ANG):
                at = a * TILE + c * UC
                own = jnp.where(owner == a, every[at:at + UC], own)
            r_ref[c, alpha] = own.astype(bf16)
            for n in range(na - 1):
                send(a_copy(phase, c, n, r_ref.at[c, alpha], r_ref.at[c, alpha]))

    def a_wait(phase, c, ref_of):
        for n, step in enumerate(a_steps):
            ref = ref_of(n, a_at(-step))
            a_copy(phase, c, n, ref, ref).wait_recv()

    def b_wait(phase, c, ref_of):
        for n, step in enumerate(b_steps):
            ref = ref_of(n, b_at((-step[0], -step[1])))
            b_copy(phase, c, n, ref, ref).wait_recv()

    near_copy.wait_recv()
    pl.when(far_valid)(far_copy.wait_recv)
    measured = meas_ref[...]
    beside, beyond = near_ref[...], far_ref[...].astype(f32)
    below = jnp.where(odd == 1, beside, beyond)
    above = jnp.where(odd == 1, beyond, beside)
    send_responses(1, r1_ref, back_of(below, measured, above))

    a_wait(0, 0, lambda n, at: meta_recv.at[at])
    near = jnp.concatenate([meta_recv[a, 0:nb, :] for a in range(na)], axis=0).astype(bf16)
    e_row, e_col = iota((TILE, TILE), 0), iota((TILE, TILE), 1)
    same = (e_row >> 4) == (e_col >> 4)
    for i in range(TILES):
        expand = jnp.logical_and(same, (e_row & (TILES - 1)) == i).astype(f32).astype(bf16)
        x_ref[i] = mm(near, expand)
    tile_lane = (iota((BASIS, TILE), 1) & (TILES - 1)).astype(f32)
    phi_high, phi_low = [], []
    for a in range(na):
        value = meta_recv[a, 8:16, :]
        high = value.astype(bf16).astype(f32)
        phi_high.append(high)
        phi_low.append(value - high)

    def build(b, carry):
        for pair in range(TILES // 2):
            for a in range(na):
                high, low = [], []
                for i in (2 * pair, 2 * pair + 1):
                    line = x_ref[i, pl.ds(a * nb + b, 1), :]
                    hit = jnp.broadcast_to(line, (BASIS, TILE)) == tile_lane
                    high.append(jnp.where(hit, phi_high[a], 0.0))
                    low.append(jnp.where(hit, phi_low[a], 0.0))
                at = pl.ds(pl.multiple_of(b * TILE + pair * 16, 16), 16)
                m_ref[at, a * TILE:(a + 1) * TILE] = jnp.concatenate(high, axis=0).astype(bf16)
                if SPLIT_PHI:
                    ml_ref[at, a * TILE:(a + 1) * TILE] = jnp.concatenate(low, axis=0).astype(bf16)
        return carry

    lax.fori_loop(0, nb, build, 0)

    def wide(ref, c, count):
        return jnp.concatenate([ref[c, j] for j in range(count)], axis=1)

    def scatter_gradient(phase, a_phase, r_ref, p_send, p_recv, use):
        gathered = []

        def rows_of(c, b):
            at = pl.ds(pl.multiple_of(b * TILE, TILE), TILE)
            value = mm(gathered[c], m_ref[at, :], NT)
            if SPLIT_PHI:
                value = value + mm(gathered[c], ml_ref[at, :], NT)
            return value

        for c in range(CHUNKS):
            a_wait(a_phase, c, lambda n, at: r_ref.at[c, at])
            gathered.append(wide(r_ref, c, na))
            for n, step in enumerate(b_steps):
                p_send[c, n] = rows_of(c, b_at(step)).astype(bf16)
                send(b_copy(phase, c, n, p_send.at[c, n], p_recv.at[c, n]))
        own = [rows_of(c, beta) for c in range(CHUNKS)]
        for c in range(CHUNKS):
            b_wait(phase, c, lambda n, at: p_recv.at[c, n])
            total = own[c]
            for n in range(nb - 1):
                total = total + p_recv[c, n].astype(f32)
            use(c, total)

    firsts = []

    def use_first(c, total):
        first = (STEP * total).astype(bf16)
        firsts.append(first.astype(f32))
        first_ref[c, beta] = first
        for n in range(nb - 1):
            send(b_copy(1, c, n, first_ref.at[c, beta], first_ref.at[c, beta]))

    scatter_gradient(0, 1, r1_ref, p1_send, p1_recv, use_first)
    fields = []

    def sums_of(c, a):
        at = pl.ds(pl.multiple_of(a * TILE, TILE), TILE)
        value = mm(fields[c], m_ref[:, at])
        if SPLIT_PHI:
            value = value + mm(fields[c], ml_ref[:, at])
        return value

    for c in range(CHUNKS):
        b_wait(1, c, lambda n, at: first_ref.at[c, at])
        fields.append(wide(first_ref, c, nb))
        for n, step in enumerate(a_steps):
            s_send[c, n] = sums_of(c, a_at(step)).astype(bf16)
            send(a_copy(2, c, n, s_send.at[c, n], s_recv.at[c, n]))
    sums = [sums_of(c, alpha) for c in range(CHUNKS)]
    landed = jnp.zeros((TILE, 2 * TILE), f32)
    for c in range(CHUNKS):
        a_wait(2, c, lambda n, at: s_recv.at[c, n])
        total = sums[c]
        for n in range(na - 1):
            total = total + s_recv[c, n].astype(f32)
        some = jnp.concatenate([w_ref[a, c * UC:(c + 1) * UC, :] for a in range(ANG)], axis=0)
        owner = jnp.broadcast_to(slot_lane[:1], (UC, TILE))
        masked = jnp.concatenate([jnp.where(owner == a, total, 0.0) for a in range(ANG)], axis=0)
        for half in split(masked.T):
            landed = landed + mm(half, some)
    plane = landed[:, :TILE] + shift_down(landed[:, TILE:])
    plane_ref[...] = plane.astype(bf16)
    for step in SLAB_OFFS:
        send(z_copy(step), z_valid(step))
    for step in SLAB_OFFS:
        pl.when(z_valid(step))(z_arrival(step).wait_recv)
    planes = {step: planes_ref[z_index(step)].astype(f32) for step in SLAB_OFFS}
    planes[0] = plane
    seen = {-1: below, 0: measured, 1: above}

    def misfit_at(v):
        return jnp.concatenate([
            cone(0, v, p) * part(planes[v - 1], p) + cone(1, v, p) * part(planes[v], p)
            + cone(2, v, p) * part(planes[v + 1], p) - part(seen[v], p)
            for p in range(PROJ)
        ], axis=0)

    misfit = misfit_at(0)
    misfit_ref[...] = misfit

    send_responses(3, r2_ref, back_of(misfit_at(-1), misfit, misfit_at(1)))
    updates = []
    scatter_gradient(2, 3, r2_ref, p2_send, p2_recv, lambda c, total: updates.append(total))
    rows_now = jnp.concatenate(
        [first - STEP * update for first, update in zip(firsts, updates)], axis=0
    ).T.astype(bf16)
    coef_ref[...] = jnp.concatenate(
        [rows_now[i * BASIS:(i + 1) * BASIS] for i in range(TILES)], axis=1
    )

    finish()


def local(grid, slabs, measured, basis_time, frame_index, angle_slot, proj_weights, tile_offsets, cone_weights):
    ny, nz, nx = grid
    na, nb = nz, ny * nx
    block, chunk = (TILE, TILE), (UC, TILE)
    vmem = pl.BlockSpec(memory_space=pltpu.VMEM)
    hbm = pl.BlockSpec(memory_space=pltpu.HBM)
    coefficients, misfit = pl.pallas_call(
        functools.partial(kernel, grid, slabs),
        out_shape=(
            pltpu.VMEM((BASIS, TILES * TILE), bf16),
            pltpu.VMEM(block, f32),
        ),
        in_specs=[hbm] * 7,
        out_specs=(vmem, vmem),
        scratch_shapes=[
            pltpu.VMEM(block, f32),
            pltpu.VMEM((BASIS, 32), f32),
            pltpu.SMEM((PROJ,), i32),
            pltpu.SMEM((PROJ,), i32),
            pltpu.VMEM((ANG, TILE, 2 * TILE), bf16),
            pltpu.VMEM((ANG, TILES, na * nb), i32),
            pltpu.SMEM((3, slabs, PROJ), f32),
            pltpu.SemaphoreType.DMA((7,)),
            pltpu.VMEM((na, 16, TILE), f32),
            pltpu.VMEM((na, 16, TILE), f32),
            pltpu.VMEM((TILES, na * nb, TILE), f32),
            pltpu.VMEM((nb * TILE, na * TILE), bf16),
            pltpu.VMEM((nb * TILE, na * TILE), bf16),
            pltpu.VMEM(block, f32),
            pltpu.VMEM(block, bf16),
            pltpu.VMEM(block, bf16),
            pltpu.VMEM(block, bf16),
            pltpu.VMEM((4,) + block, bf16),
            pltpu.VMEM((CHUNKS, na) + chunk, bf16),
            pltpu.VMEM((CHUNKS, na) + chunk, bf16),
            pltpu.VMEM((CHUNKS, nb - 1) + chunk, bf16),
            pltpu.VMEM((CHUNKS, nb - 1) + chunk, bf16),
            pltpu.VMEM((CHUNKS, nb - 1) + chunk, bf16),
            pltpu.VMEM((CHUNKS, nb - 1) + chunk, bf16),
            pltpu.VMEM((CHUNKS, nb) + chunk, bf16),
            pltpu.VMEM((CHUNKS, na - 1) + chunk, bf16),
            pltpu.VMEM((CHUNKS, na - 1) + chunk, bf16),
            pltpu.SemaphoreType.DMA((4, CHUNKS, na - 1)),
            pltpu.SemaphoreType.DMA((4, CHUNKS, na - 1)),
            pltpu.SemaphoreType.DMA((3, CHUNKS, nb - 1)),
            pltpu.SemaphoreType.DMA((3, CHUNKS, nb - 1)),
            pltpu.SemaphoreType.DMA((4,)),
            pltpu.SemaphoreType.DMA((4,)),
            pltpu.SemaphoreType.DMA((2,)),
            pltpu.SemaphoreType.DMA((2,)),
        ],
        compiler_params=pltpu.CompilerParams(
            collective_id=0, has_side_effects=True, vmem_limit_bytes=62 * 1000 * 1000
        ),
        name="two_gradients",
    )(
        measured.reshape(block),
        basis_time.T,
        frame_index,
        angle_slot,
        proj_weights,
        tile_offsets.transpose(0, 2, 1),
        cone_weights.transpose(0, 2, 1),
    )
    return (
        coefficients.reshape(1, BASIS, 1, TILES * TILE),
        misfit.reshape(PROJ, 1, TILES * TILE),
    )


def solution(mesh):
    placed = (
        P("angle", "zslab", None),
        P(),
        P("angle"),
        P("angle"),
        P("angle", None, None),
        P("angle", None, None),
        P(None, "angle", None),
    )
    grid = GRIDS[mesh.shape["angle"]]
    return jax.shard_map(
        functools.partial(local, grid, mesh.shape["zslab"]),
        mesh=mesh,
        in_specs=placed,
        out_specs=(P("angle", None, "zslab", None), P("angle", "zslab", None)),
        check_vma=False,
    )
```

```python
import functools

import jax
import jax.numpy as jnp
from jax import lax
from jax.experimental import pallas as pl
from jax.experimental.pallas import tpu as pltpu
from jax.sharding import PartitionSpec as P

GRIDS = {64: (4, 8, 2), 8: (2, 2, 2)}
MESH = pl.DeviceIdType.MESH
STEP = 0.4
TILE = 128
BASIS = 8
PROJ = 8
ANG = 4
TILES = 16
VIEWS = 2
UC = TILE // VIEWS
f32, bf16, i32 = jnp.float32, jnp.bfloat16, jnp.int32
SLAB_OFFS = (-2, 2, -1, 1)

NN = (((1,), (0,)), ((), ()))
NT = (((1,), (1,)), ((), ()))


def mm(a, b, dims=NN):
    return lax.dot_general(a, b, dims, preferred_element_type=f32)


def split(value):
    high = value.astype(bf16)
    return high, (value - high.astype(f32)).astype(bf16)


def iota(shape, dim):
    return lax.broadcasted_iota(i32, shape, dim)


def kernel(
    grid, slabs,
    meas_hbm, basis_hbm, frame_hbm, slot_hbm, w_hbm, off_hbm, cone_hbm,
    coef_ref, misfit_ref,
    meas_ref, basis_ref, frame_ref, slot_ref, w_ref, off_ref, cone_ref, load_sem,
    meta_send, meta_recv, x_ref, ma_ref, mb_ref, near_ref, edge_ref, far_ref, plane_ref, planes_ref,
    r1_ref, r2_ref, p1_send, p1_recv, p2_send, p2_recv, first_ref, s_send, s_recv,
    g_ss, g_rs, c_ss, c_rs, z_ss, z_rs, h_ss, h_rs,
):
    ny, nz, nx = grid
    na, nb = nz, ny * nx
    slab = lax.axis_index("zslab")
    place = lax.axis_index("angle")
    my_x = place % nx
    alpha = (place // nx) % nz
    my_y = place // (nx * nz)
    beta = my_y * nx + my_x

    a_steps = sorted(range(1, na), key=lambda d: -min(d, na - d))
    b_steps = sorted(
        [(dy, dx) for dy in range(ny) for dx in range(nx) if dy or dx],
        key=lambda s: -(min(s[0], ny - s[0]) + s[1]),
    )

    def a_at(step):
        return lax.rem(alpha + step + na, na)

    def a_device(step):
        return my_y * (nz * nx) + a_at(step) * nx + my_x

    def b_at(step):
        return lax.rem(my_y + step[0] + ny, ny) * nx + lax.rem(my_x + step[1] + nx, nx)

    def b_device(step):
        other = b_at(step)
        return (other // nx) * (nz * nx) + alpha * nx + other % nx

    groups = (
        (na, alpha, a_steps, a_at, a_device, lambda step: -step),
        (nb, beta, b_steps, b_at, b_device, lambda step: (-step[0], -step[1])),
    )
    m_refs = (ma_ref, mb_ref)

    def copy(kind, v, phase, n, src, dst):
        _, _, steps, _, device, _ = groups[(v + kind) % 2]
        ss, rs = (g_ss, g_rs) if kind == 0 else (c_ss, c_rs)
        return pltpu.make_async_remote_copy(
            src_ref=src, dst_ref=dst, send_sem=ss.at[v, phase, n], recv_sem=rs.at[v, phase, n],
            device_id={"angle": device(steps[n])}, device_id_type=MESH,
        )

    def wait_all(kind, v, phase, ref_of):
        _, _, steps, at, _, opposite = groups[(v + kind) % 2]
        for n, step in enumerate(steps):
            ref = ref_of(n, at(opposite(step)))
            copy(kind, v, phase, n, ref, ref).wait_recv()

    def z_valid(step):
        return jnp.logical_and(slab + step >= 0, slab + step < slabs)

    def z_index(step):
        return SLAB_OFFS.index(step)

    def z_copy(step):
        back_slot = z_index(-step)
        return pltpu.make_async_remote_copy(
            src_ref=plane_ref, dst_ref=planes_ref.at[back_slot], send_sem=z_ss.at[z_index(step)],
            recv_sem=z_rs.at[back_slot], device_id={"zslab": slab + step}, device_id_type=MESH,
        )

    def z_arrival(step):
        slot = z_index(step)
        return pltpu.make_async_remote_copy(
            src_ref=plane_ref, dst_ref=planes_ref.at[slot], send_sem=z_ss.at[slot],
            recv_sem=z_rs.at[slot], device_id={"zslab": slab + step}, device_id_type=MESH,
        )

    odd = slab % 2
    near_copy = pltpu.make_async_remote_copy(
        src_ref=meas_ref, dst_ref=near_ref, send_sem=h_ss.at[0], recv_sem=h_rs.at[0],
        device_id={"zslab": slab + 1 - 2 * odd}, device_id_type=MESH,
    )
    far_step = 2 * odd - 1
    far_valid = jnp.logical_and(slab + far_step >= 0, slab + far_step < slabs)
    far_copy = pltpu.make_async_remote_copy(
        src_ref=edge_ref, dst_ref=far_ref, send_sem=h_ss.at[1], recv_sem=h_rs.at[1],
        device_id={"zslab": slab + far_step}, device_id_type=MESH,
    )

    loads = [
        pltpu.make_async_copy(source, target, load_sem.at[n])
        for n, (source, target) in enumerate([
            (slot_hbm, slot_ref), (off_hbm, off_ref), (frame_hbm, frame_ref), (basis_hbm, basis_ref),
            (meas_hbm, meas_ref), (cone_hbm, cone_ref), (w_hbm, w_ref),
        ])
    ]
    for load in loads:
        load.start()

    sent = []

    def send(copy, valid=None):
        if valid is None:
            copy.start()
        else:
            pl.when(valid)(copy.start)
        sent.append((copy, valid))

    def finish():
        for copy, valid in sent:
            if valid is None:
                copy.wait_send()
            else:
                pl.when(valid)(copy.wait_send)

    barrier = pltpu.get_barrier_semaphore()
    for step in a_steps:
        pl.semaphore_signal(barrier, inc=1, device_id={"angle": a_device(step)}, device_id_type=MESH)
    for step in b_steps:
        pl.semaphore_signal(barrier, inc=1, device_id={"angle": b_device(step)}, device_id_type=MESH)
    for step in range(1, slabs):
        pl.semaphore_signal(
            barrier, inc=1, device_id={"zslab": lax.rem(slab + step, slabs)}, device_id_type=MESH
        )

    for load in loads[:4]:
        load.wait()
    slots = [slot_ref[p] for p in range(PROJ)]
    rows = iota((PROJ * TILES, ANG * TILES), 0)
    cols = iota((PROJ * TILES, ANG * TILES), 1)
    slot_rows = jnp.concatenate(
        [jnp.full((TILES, ANG * TILES), slots[p], i32) for p in range(PROJ)], axis=0
    )
    pick = jnp.logical_and((rows & (TILES - 1)) == (cols & (TILES - 1)), slot_rows == (cols >> 4))
    offs = off_ref[...].reshape(ANG * TILES, na * nb).astype(f32).astype(bf16)
    offs_p = mm(pick.astype(f32).astype(bf16), offs)
    offs_sent = []
    order = iota((na * nb, na * nb), 0)
    for o_alpha, o_beta in ((order // nb, order % nb), (order % na, order // na)):
        image_row = (o_beta // nx) * (nz * nx) + o_alpha * nx + o_beta % nx
        permute = (image_row == iota((na * nb, na * nb), 1)).astype(f32).astype(bf16)
        offs_sent.append(mm(permute, offs_p.astype(bf16), NT))

    lane_p = iota((32, TILE), 1) >> 4
    frames = jnp.zeros((32, TILE), i32)
    for p in range(PROJ):
        frames = jnp.where(lane_p == p, frame_ref[p], frames)
    hot = (frames == iota((32, TILE), 0)).astype(f32)
    phi = lax.dot_general(
        basis_ref[...], hot, NN, precision=lax.Precision.HIGHEST, preferred_element_type=f32
    )
    for v in range(VIEWS):
        (ng, me, *_), (ns, *_) = groups[v], groups[1 - v]
        for g in range(ng):
            meta_send[v, g, 0:ns, :] = offs_sent[v][g * ns:(g + 1) * ns]
            meta_send[v, g, 8:16, :] = phi
        meta_recv[v, me] = meta_send[v, me]

    for step in SLAB_OFFS:
        @pl.when(jnp.logical_not(z_valid(step)))
        def _():
            planes_ref[z_index(step)] = jnp.zeros((TILE, TILE), bf16)

    @pl.when(jnp.logical_not(far_valid))
    def _():
        far_ref[...] = jnp.zeros((TILE, TILE), bf16)

    for load in loads[4:]:
        load.wait()
    edge_ref[...] = meas_ref[...].astype(bf16)
    pl.semaphore_wait(barrier, len(a_steps) + len(b_steps) + slabs - 1)

    send(far_copy, far_valid)
    send(near_copy)
    for v in range(VIEWS):
        _, me, steps, at, _, _ = groups[v]
        for n, step in enumerate(steps):
            send(copy(0, v, 0, n, meta_send.at[v, at(step)], meta_recv.at[v, me]))

    def cone(kind, step, p):
        at = jnp.clip(slab + step, 0, slabs - 1)
        return cone_ref[kind, at, p]

    def cone_masked(kind, step, p):
        return jnp.where(z_valid(step), cone(kind, step, p), 0.0)

    def part(value, p):
        return value[p * TILES:(p + 1) * TILES]

    def back_of(below, here, above):
        return jnp.concatenate([
            cone_masked(0, 1, p) * part(above, p) + cone(1, 0, p) * part(here, p)
            + cone_masked(2, -1, p) * part(below, p)
            for p in range(PROJ)
        ], axis=0)

    def shift_up(value):
        return jnp.concatenate([value[1:], value[:1]], axis=0)

    def shift_down(value):
        return jnp.concatenate([value[-1:], value[:-1]], axis=0)

    weights = w_ref[...].reshape(ANG * TILE, 2 * TILE)
    slot_lane = jnp.concatenate(
        [jnp.full((8, TILES), slots[p], i32) for p in range(PROJ)], axis=1
    )

    def send_responses(phase, r_ref, back):
        high, low = split(jnp.concatenate([back, shift_up(back)], axis=1))
        every = mm(weights, high, NT) + mm(weights, low, NT)
        owner = jnp.broadcast_to(slot_lane[:1], (UC, TILE))
        for v in range(VIEWS):
            ng, me, *_ = groups[v]
            own = jnp.zeros((UC, TILE), f32)
            for a in range(ANG):
                at = a * TILE + v * UC
                own = jnp.where(owner == a, every[at:at + UC], own)
            r_ref[v, me] = own.astype(bf16)
            for n in range(ng - 1):
                send(copy(0, v, phase, n, r_ref.at[v, me], r_ref.at[v, me]))

    near_copy.wait_recv()
    pl.when(far_valid)(far_copy.wait_recv)
    measured = meas_ref[...]
    beside, beyond = near_ref[...], far_ref[...].astype(f32)
    below = jnp.where(odd == 1, beside, beyond)
    above = jnp.where(odd == 1, beyond, beside)
    send_responses(1, r1_ref, back_of(below, measured, above))

    e_row, e_col = iota((TILE, TILE), 0), iota((TILE, TILE), 1)
    same = (e_row >> 4) == (e_col >> 4)
    tile_lane = (iota((BASIS, TILE), 1) & (TILES - 1)).astype(f32)
    for v in (1, 0):
        (ng, *_), (ns, *_), m_ref = groups[v], groups[1 - v], m_refs[v]
        wait_all(0, v, 0, lambda n, at: meta_recv.at[v, at])
        near = jnp.concatenate([meta_recv[v, g, 0:ns, :] for g in range(ng)], axis=0).astype(bf16)
        for i in range(TILES):
            expand = jnp.logical_and(same, (e_row & (TILES - 1)) == i).astype(f32).astype(bf16)
            x_ref[v, i] = mm(near, expand)
        factors = [meta_recv[v, g, 8:16, :] for g in range(ng)]

        def build(b, carry):
            for pair in range(TILES // 2):
                for g in range(ng):
                    lines = []
                    for i in (2 * pair, 2 * pair + 1):
                        line = x_ref[v, i, pl.ds(g * ns + b, 1), :]
                        hit = jnp.broadcast_to(line, (BASIS, TILE)) == tile_lane
                        lines.append(jnp.where(hit, factors[g], 0.0))
                    at = pl.ds(pl.multiple_of(b * TILE + pair * 16, 16), 16)
                    m_ref[at, g * TILE:(g + 1) * TILE] = jnp.concatenate(lines, axis=0).astype(bf16)
            return carry

        lax.fori_loop(0, ns, build, 0)

    def wide(ref, c, count):
        return jnp.concatenate([ref[c, j] for j in range(count)], axis=1)

    def scatter_gradient(phase, g_phase, r_ref, p_send, p_recv, use):
        gathered = {}

        def rows_of(v, pair):
            some = jnp.concatenate(
                [m_refs[v][pl.ds(pl.multiple_of(b * TILE, TILE), TILE), :] for b in pair], axis=0
            )
            value = mm(gathered[v], some, NT)
            return value[:, :TILE], value[:, TILE:]

        own = {}
        for v in (1, 0):
            (ng, *_), (_, _, steps, at_of, _, _) = groups[v], groups[1 - v]
            wait_all(0, v, g_phase, lambda n, at: r_ref.at[v, at])
            gathered[v] = wide(r_ref, v, ng)
            places = [at_of(step) for step in steps] + [groups[1 - v][1]]
            for n in range(0, len(places), 2):
                for m, value in zip((n, n + 1), rows_of(v, places[n:n + 2])):
                    if m == len(steps):
                        own[v] = value
                        continue
                    p_send[v, m] = value.astype(bf16)
                    send(copy(1, v, phase, m, p_send.at[v, m], p_recv.at[v, m]))
        for v in (0, 1):
            wait_all(1, v, phase, lambda n, at: p_recv.at[v, n])
            total = own[v]
            for n in range(groups[1 - v][0] - 1):
                total = total + p_recv[v, n].astype(f32)
            use(v, total)

    firsts = []

    def use_first(v, total):
        ns, me, *_ = groups[1 - v]
        first = (STEP * total).astype(bf16)
        firsts.append(first.astype(f32))
        first_ref[v, me] = first
        for n in range(ns - 1):
            send(copy(1, v, 1, n, first_ref.at[v, me], first_ref.at[v, me]))

    scatter_gradient(0, 1, r1_ref, p1_send, p1_recv, use_first)
    fields = []

    def sums_of(v, pair):
        some = jnp.concatenate(
            [m_refs[v][:, pl.ds(pl.multiple_of(g * TILE, TILE), TILE)] for g in pair], axis=1
        )
        value = mm(fields[v], some)
        return value[:, :TILE], value[:, TILE:]

    sums = {}
    for v in (0, 1):
        (_, _, steps, at_of, _, _), (ns, *_) = groups[v], groups[1 - v]
        wait_all(1, v, 1, lambda n, at: first_ref.at[v, at])
        fields.append(wide(first_ref, v, ns))
        places = [at_of(step) for step in steps] + [groups[v][1]]
        for n in range(0, len(places), 2):
            for m, value in zip((n, n + 1), sums_of(v, places[n:n + 2])):
                if m == len(steps):
                    sums[v] = value
                    continue
                s_send[v, m] = value.astype(bf16)
                send(copy(0, v, 2, m, s_send.at[v, m], s_recv.at[v, m]))
    landed = jnp.zeros((TILE, 2 * TILE), f32)
    for v in (0, 1):
        wait_all(0, v, 2, lambda n, at: s_recv.at[v, n])
        total = sums[v]
        for n in range(groups[v][0] - 1):
            total = total + s_recv[v, n].astype(f32)
        some = jnp.concatenate([w_ref[a, v * UC:(v + 1) * UC, :] for a in range(ANG)], axis=0)
        owner = jnp.broadcast_to(slot_lane[:1], (UC, TILE))
        masked = jnp.concatenate([jnp.where(owner == a, total, 0.0) for a in range(ANG)], axis=0)
        for half in split(masked.T):
            landed = landed + mm(half, some)
    plane = landed[:, :TILE] + shift_down(landed[:, TILE:])
    plane_ref[...] = plane.astype(bf16)
    for step in SLAB_OFFS:
        send(z_copy(step), z_valid(step))
    for step in SLAB_OFFS:
        pl.when(z_valid(step))(z_arrival(step).wait_recv)
    planes = {step: planes_ref[z_index(step)].astype(f32) for step in SLAB_OFFS}
    planes[0] = plane
    seen = {-1: below, 0: measured, 1: above}

    def misfit_at(v):
        return jnp.concatenate([
            cone(0, v, p) * part(planes[v - 1], p) + cone(1, v, p) * part(planes[v], p)
            + cone(2, v, p) * part(planes[v + 1], p) - part(seen[v], p)
            for p in range(PROJ)
        ], axis=0)

    misfit = misfit_at(0)
    misfit_ref[...] = misfit

    send_responses(3, r2_ref, back_of(misfit_at(-1), misfit, misfit_at(1)))
    updates = []
    scatter_gradient(2, 3, r2_ref, p2_send, p2_recv, lambda v, total: updates.append(total))
    rows_now = jnp.concatenate(
        [first - STEP * update for first, update in zip(firsts, updates)], axis=0
    ).T.astype(bf16)
    coef_ref[...] = jnp.concatenate(
        [rows_now[i * BASIS:(i + 1) * BASIS] for i in range(TILES)], axis=1
    )

    finish()


def local(grid, slabs, measured, basis_time, frame_index, angle_slot, proj_weights, tile_offsets, cone_weights):
    ny, nz, nx = grid
    na, nb = nz, ny * nx
    most = max(na, nb)
    block, blocks = (TILE, TILE), (VIEWS, most, UC, TILE)
    vmem = pl.BlockSpec(memory_space=pltpu.VMEM)
    hbm = pl.BlockSpec(memory_space=pltpu.HBM)
    coefficients, misfit = pl.pallas_call(
        functools.partial(kernel, grid, slabs),
        out_shape=(
            pltpu.VMEM((BASIS, TILES * TILE), bf16),
            pltpu.VMEM(block, f32),
        ),
        in_specs=[hbm] * 7,
        out_specs=(vmem, vmem),
        scratch_shapes=[
            pltpu.VMEM(block, f32),
            pltpu.VMEM((BASIS, 32), f32),
            pltpu.SMEM((PROJ,), i32),
            pltpu.SMEM((PROJ,), i32),
            pltpu.VMEM((ANG, TILE, 2 * TILE), bf16),
            pltpu.VMEM((ANG, TILES, na * nb), i32),
            pltpu.SMEM((3, slabs, PROJ), f32),
            pltpu.SemaphoreType.DMA((7,)),
            pltpu.VMEM((VIEWS, most, 16, TILE), f32),
            pltpu.VMEM((VIEWS, most, 16, TILE), f32),
            pltpu.VMEM((VIEWS, TILES, na * nb, TILE), f32),
            pltpu.VMEM((nb * TILE, na * TILE), bf16),
            pltpu.VMEM((na * TILE, nb * TILE), bf16),
            pltpu.VMEM(block, f32),
            pltpu.VMEM(block, bf16),
            pltpu.VMEM(block, bf16),
            pltpu.VMEM(block, bf16),
            pltpu.VMEM((4,) + block, bf16),
            pltpu.VMEM(blocks, bf16),
            pltpu.VMEM(blocks, bf16),
            pltpu.VMEM(blocks, bf16),
            pltpu.VMEM(blocks, bf16),
            pltpu.VMEM(blocks, bf16),
            pltpu.VMEM(blocks, bf16),
            pltpu.VMEM(blocks, bf16),
            pltpu.VMEM(blocks, bf16),
            pltpu.VMEM(blocks, bf16),
            pltpu.SemaphoreType.DMA((VIEWS, 4, most - 1)),
            pltpu.SemaphoreType.DMA((VIEWS, 4, most - 1)),
            pltpu.SemaphoreType.DMA((VIEWS, 3, most - 1)),
            pltpu.SemaphoreType.DMA((VIEWS, 3, most - 1)),
            pltpu.SemaphoreType.DMA((4,)),
            pltpu.SemaphoreType.DMA((4,)),
            pltpu.SemaphoreType.DMA((2,)),
            pltpu.SemaphoreType.DMA((2,)),
        ],
        compiler_params=pltpu.CompilerParams(
            collective_id=0, has_side_effects=True, vmem_limit_bytes=62 * 1000 * 1000
        ),
        name="two_gradients",
    )(
        measured.reshape(block),
        basis_time.T,
        frame_index,
        angle_slot,
        proj_weights,
        tile_offsets.transpose(0, 2, 1),
        cone_weights.transpose(0, 2, 1),
    )
    return (
        coefficients.reshape(1, BASIS, 1, TILES * TILE),
        misfit.reshape(PROJ, 1, TILES * TILE),
    )


def solution(mesh):
    placed = (
        P("angle", "zslab", None),
        P(),
        P("angle"),
        P("angle"),
        P("angle", None, None),
        P("angle", None, None),
        P(None, "angle", None),
    )
    grid = GRIDS[mesh.shape["angle"]]
    return jax.shard_map(
        functools.partial(local, grid, mesh.shape["zslab"]),
        mesh=mesh,
        in_specs=placed,
        out_specs=(P("angle", None, "zslab", None), P("angle", "zslab", None)),
        check_vma=False,
    )
```

```python
import functools

import jax
import jax.numpy as jnp
from jax import lax
from jax.experimental import pallas as pl
from jax.experimental.pallas import tpu as pltpu
from jax.sharding import PartitionSpec as P

GRIDS = {64: (4, 8, 2), 8: (2, 2, 2)}
MESH = pl.DeviceIdType.MESH
STEP = 0.4
TILE = 128
BASIS = 8
PROJ = 8
ANG = 4
TILES = 16
VIEWS = 2
UC = TILE // VIEWS
f32, bf16, i32 = jnp.float32, jnp.bfloat16, jnp.int32
SLAB_OFFS = (-2, 2, -1, 1)

NN = (((1,), (0,)), ((), ()))
NT = (((1,), (1,)), ((), ()))


def mm(a, b, dims=NN):
    return lax.dot_general(a, b, dims, preferred_element_type=f32)


def split(value):
    high = value.astype(bf16)
    return high, (value - high.astype(f32)).astype(bf16)


def iota(shape, dim):
    return lax.broadcasted_iota(i32, shape, dim)


def kernel(
    grid, slabs,
    meas_hbm, basis_hbm, frame_hbm, slot_hbm, w_hbm, off_hbm, cone_hbm,
    coef_ref, misfit_ref,
    meas_ref, basis_ref, frame_ref, slot_ref, w_ref, off_ref, cone_ref, load_sem,
    meta_send, meta_recv, x_ref, xt_ref, ma_ref, mb_ref, mta_ref, mtb_ref, near_ref, edge_ref, far_ref, plane_ref, planes_ref,
    r1_ref, r2_ref, p1_send, p1_recv, p2_send, p2_recv, first_ref, s_send, s_recv,
    g_ss, g_rs, c_ss, c_rs, z_ss, z_rs, h_ss, h_rs,
):
    ny, nz, nx = grid
    na, nb = nz, ny * nx
    slab = lax.axis_index("zslab")
    place = lax.axis_index("angle")
    my_x = place % nx
    alpha = (place // nx) % nz
    my_y = place // (nx * nz)
    beta = my_y * nx + my_x

    a_steps = sorted(range(1, na), key=lambda d: -min(d, na - d))
    b_steps = sorted(
        [(dy, dx) for dy in range(ny) for dx in range(nx) if dy or dx],
        key=lambda s: -(min(s[0], ny - s[0]) + s[1]),
    )

    def a_at(step):
        return lax.rem(alpha + step + na, na)

    def a_device(step):
        return my_y * (nz * nx) + a_at(step) * nx + my_x

    def b_at(step):
        return lax.rem(my_y + step[0] + ny, ny) * nx + lax.rem(my_x + step[1] + nx, nx)

    def b_device(step):
        other = b_at(step)
        return (other // nx) * (nz * nx) + alpha * nx + other % nx

    groups = (
        (na, alpha, a_steps, a_at, a_device, lambda step: -step),
        (nb, beta, b_steps, b_at, b_device, lambda step: (-step[0], -step[1])),
    )
    m_refs, mt_refs = (ma_ref, mb_ref), (mta_ref, mtb_ref)

    def copy(kind, v, phase, n, src, dst):
        _, _, steps, _, device, _ = groups[(v + kind) % 2]
        ss, rs = (g_ss, g_rs) if kind == 0 else (c_ss, c_rs)
        return pltpu.make_async_remote_copy(
            src_ref=src, dst_ref=dst, send_sem=ss.at[v, phase, n], recv_sem=rs.at[v, phase, n],
            device_id={"angle": device(steps[n])}, device_id_type=MESH,
        )

    def wait_all(kind, v, phase, ref_of):
        _, _, steps, at, _, opposite = groups[(v + kind) % 2]
        for n, step in enumerate(steps):
            ref = ref_of(n, at(opposite(step)))
            copy(kind, v, phase, n, ref, ref).wait_recv()

    def z_valid(step):
        return jnp.logical_and(slab + step >= 0, slab + step < slabs)

    def z_index(step):
        return SLAB_OFFS.index(step)

    def z_copy(step):
        back_slot = z_index(-step)
        return pltpu.make_async_remote_copy(
            src_ref=plane_ref, dst_ref=planes_ref.at[back_slot], send_sem=z_ss.at[z_index(step)],
            recv_sem=z_rs.at[back_slot], device_id={"zslab": slab + step}, device_id_type=MESH,
        )

    def z_arrival(step):
        slot = z_index(step)
        return pltpu.make_async_remote_copy(
            src_ref=plane_ref, dst_ref=planes_ref.at[slot], send_sem=z_ss.at[slot],
            recv_sem=z_rs.at[slot], device_id={"zslab": slab + step}, device_id_type=MESH,
        )

    odd = slab % 2
    near_copy = pltpu.make_async_remote_copy(
        src_ref=meas_ref, dst_ref=near_ref, send_sem=h_ss.at[0], recv_sem=h_rs.at[0],
        device_id={"zslab": slab + 1 - 2 * odd}, device_id_type=MESH,
    )
    far_step = 2 * odd - 1
    far_valid = jnp.logical_and(slab + far_step >= 0, slab + far_step < slabs)
    far_copy = pltpu.make_async_remote_copy(
        src_ref=edge_ref, dst_ref=far_ref, send_sem=h_ss.at[1], recv_sem=h_rs.at[1],
        device_id={"zslab": slab + far_step}, device_id_type=MESH,
    )

    loads = [
        pltpu.make_async_copy(source, target, load_sem.at[n])
        for n, (source, target) in enumerate([
            (slot_hbm, slot_ref), (off_hbm, off_ref), (frame_hbm, frame_ref), (basis_hbm, basis_ref),
            (meas_hbm, meas_ref), (cone_hbm, cone_ref), (w_hbm, w_ref),
        ])
    ]
    sent = []

    def send(copy, valid=None):
        if valid is None:
            copy.start()
        else:
            pl.when(valid)(copy.start)
        sent.append((copy, valid))

    def finish():
        for copy, valid in sent:
            if valid is None:
                copy.wait_send()
            else:
                pl.when(valid)(copy.wait_send)

    barrier = pltpu.get_barrier_semaphore()
    for step in sorted(range(1, slabs), key=lambda d: -min(d, slabs - d)):
        pl.semaphore_signal(
            barrier, inc=1, device_id={"zslab": lax.rem(slab + step, slabs)}, device_id_type=MESH
        )
    for step in a_steps:
        pl.semaphore_signal(barrier, inc=1, device_id={"angle": a_device(step)}, device_id_type=MESH)
    for step in b_steps:
        pl.semaphore_signal(barrier, inc=1, device_id={"angle": b_device(step)}, device_id_type=MESH)
    for load in loads:
        load.start()

    for load in loads[:4]:
        load.wait()
    slots = [slot_ref[p] for p in range(PROJ)]
    rows = iota((PROJ * TILES, ANG * TILES), 0)
    cols = iota((PROJ * TILES, ANG * TILES), 1)
    slot_rows = jnp.concatenate(
        [jnp.full((TILES, ANG * TILES), slots[p], i32) for p in range(PROJ)], axis=0
    )
    pick = jnp.logical_and((rows & (TILES - 1)) == (cols & (TILES - 1)), slot_rows == (cols >> 4))
    offs = off_ref[...].reshape(ANG * TILES, na * nb).astype(f32).astype(bf16)
    offs_p = mm(pick.astype(f32).astype(bf16), offs)
    offs_sent = []
    order = iota((na * nb, na * nb), 0)
    for o_alpha, o_beta in ((order // nb, order % nb), (order % na, order // na)):
        image_row = (o_beta // nx) * (nz * nx) + o_alpha * nx + o_beta % nx
        permute = (image_row == iota((na * nb, na * nb), 1)).astype(f32).astype(bf16)
        offs_sent.append(mm(permute, offs_p.astype(bf16), NT))

    lane_p = iota((32, TILE), 1) >> 4
    frames = jnp.zeros((32, TILE), i32)
    for p in range(PROJ):
        frames = jnp.where(lane_p == p, frame_ref[p], frames)
    hot = (frames == iota((32, TILE), 0)).astype(f32)
    phi = lax.dot_general(
        basis_ref[...], hot, NN, precision=lax.Precision.HIGHEST, preferred_element_type=f32
    )
    rows_p = iota((PROJ, 32), 0)
    frames = jnp.zeros((PROJ, 32), i32)
    for p in range(PROJ):
        frames = jnp.where(rows_p == p, frame_ref[p], frames)
    hot = (frames == iota((PROJ, 32), 1)).astype(f32)
    phi_rows = lax.dot_general(
        hot, jnp.concatenate([basis_ref[...]] * TILES, axis=0), NT,
        precision=lax.Precision.HIGHEST, preferred_element_type=f32,
    )
    for v in range(VIEWS):
        (ng, me, *_), (ns, *_) = groups[v], groups[1 - v]
        for g in range(ng):
            meta_send[v, g, 0:ns, :] = offs_sent[v][g * ns:(g + 1) * ns]
            meta_send[v, g, 8:16, :] = phi
            meta_send[v, g, 16:24, :] = phi_rows
        meta_recv[v, me] = meta_send[v, me]

    for step in SLAB_OFFS:
        @pl.when(jnp.logical_not(z_valid(step)))
        def _():
            planes_ref[z_index(step)] = jnp.zeros((TILE, TILE), bf16)

    @pl.when(jnp.logical_not(far_valid))
    def _():
        far_ref[...] = jnp.zeros((TILE, TILE), bf16)

    for load in loads[4:]:
        load.wait()
    edge_ref[...] = meas_ref[...].astype(bf16)
    pl.semaphore_wait(barrier, len(a_steps) + len(b_steps) + slabs - 1)

    send(far_copy, far_valid)
    send(near_copy)
    for v in range(VIEWS):
        _, me, steps, at, _, _ = groups[v]
        for n, step in enumerate(steps):
            send(copy(0, v, 0, n, meta_send.at[v, at(step)], meta_recv.at[v, me]))

    def cone(kind, step, p):
        at = jnp.clip(slab + step, 0, slabs - 1)
        return cone_ref[kind, at, p]

    def cone_masked(kind, step, p):
        return jnp.where(z_valid(step), cone(kind, step, p), 0.0)

    def part(value, p):
        return value[p * TILES:(p + 1) * TILES]

    def back_of(below, here, above):
        return jnp.concatenate([
            cone_masked(0, 1, p) * part(above, p) + cone(1, 0, p) * part(here, p)
            + cone_masked(2, -1, p) * part(below, p)
            for p in range(PROJ)
        ], axis=0)

    def shift_up(value):
        return jnp.concatenate([value[1:], value[:1]], axis=0)

    def shift_down(value):
        return jnp.concatenate([value[-1:], value[:-1]], axis=0)

    weights = w_ref[...].reshape(ANG * TILE, 2 * TILE)
    slot_lane = jnp.concatenate(
        [jnp.full((8, TILES), slots[p], i32) for p in range(PROJ)], axis=1
    )

    def send_responses(phase, r_ref, back):
        high, low = split(jnp.concatenate([back, shift_up(back)], axis=1))
        every = mm(weights, high, NT) + mm(weights, low, NT)
        owner = jnp.broadcast_to(slot_lane[:1], (UC, TILE))
        for v in range(VIEWS):
            ng, me, *_ = groups[v]
            own = jnp.zeros((UC, TILE), f32)
            for a in range(ANG):
                at = a * TILE + v * UC
                own = jnp.where(owner == a, every[at:at + UC], own)
            r_ref[v, me] = own.astype(bf16)
            for n in range(ng - 1):
                send(copy(0, v, phase, n, r_ref.at[v, me], r_ref.at[v, me]))

    near_copy.wait_recv()
    pl.when(far_valid)(far_copy.wait_recv)
    measured = meas_ref[...]
    beside, beyond = near_ref[...], far_ref[...].astype(f32)
    below = jnp.where(odd == 1, beside, beyond)
    above = jnp.where(odd == 1, beyond, beside)
    send_responses(1, r1_ref, back_of(below, measured, above))

    e_row, e_col = iota((TILE, TILE), 0), iota((TILE, TILE), 1)
    same = (e_row >> 4) == (e_col >> 4)
    tile_row = iota((TILES, TILE), 0).astype(f32)
    tile_lane = (iota((BASIS, TILE), 1) & (TILES - 1)).astype(f32)
    for v in (1, 0):
        (ng, *_), (ns, *_), m_ref = groups[v], groups[1 - v], m_refs[v]
        wait_all(0, v, 0, lambda n, at: meta_recv.at[v, at])
        near = jnp.concatenate([meta_recv[v, g, 0:ns, :] for g in range(ng)], axis=0).astype(bf16)
        for i in range(TILES):
            expand = jnp.logical_and(same, (e_row & (TILES - 1)) == i).astype(f32).astype(bf16)
            x_ref[v, i] = mm(near, expand)
        for p in range(PROJ):
            expand = jnp.logical_and(e_row >> 4 == p, (e_row & (TILES - 1)) == (e_col >> 3))
            xt_ref[v, p] = mm(near, expand.astype(f32).astype(bf16))
        factors = [meta_recv[v, g, 8:16, :] for g in range(ng)]

        def build(b, carry):
            for pair in range(TILES // 2):
                for g in range(ng):
                    lines = []
                    for i in (2 * pair, 2 * pair + 1):
                        line = x_ref[v, i, pl.ds(g * ns + b, 1), :]
                        hit = jnp.broadcast_to(line, (BASIS, TILE)) == tile_lane
                        lines.append(jnp.where(hit, factors[g], 0.0))
                    at = pl.ds(pl.multiple_of(b * TILE + pair * 16, 16), 16)
                    m_ref[at, g * TILE:(g + 1) * TILE] = jnp.concatenate(lines, axis=0).astype(bf16)
            at = pl.ds(pl.multiple_of(b * TILE, TILE), TILE)
            for g in range(ng):
                for p in range(PROJ):
                    line = xt_ref[v, p, pl.ds(g * ns + b, 1), :]
                    hit = jnp.broadcast_to(line, (TILES, TILE)) == tile_row
                    factor = jnp.broadcast_to(meta_recv[v, g, 16 + p:17 + p, :], (TILES, TILE))
                    mt_refs[v][g * TILE + p * TILES:g * TILE + (p + 1) * TILES, at] = jnp.where(
                        hit, factor, 0.0
                    ).astype(bf16)
            return carry

        lax.fori_loop(0, ns, build, 0)

    def wide(ref, c, count):
        return jnp.concatenate([ref[c, j] for j in range(count)], axis=1)

    def scatter_gradient(phase, g_phase, r_ref, p_send, p_recv, use):
        gathered = {}

        def rows_of(v, pair):
            some = jnp.concatenate(
                [mt_refs[v][:, pl.ds(pl.multiple_of(b * TILE, TILE), TILE)] for b in pair], axis=1
            )
            value = mm(gathered[v], some)
            return value[:, :TILE], value[:, TILE:]

        own = {}
        for v in (1, 0):
            (ng, *_), (_, _, steps, at_of, _, _) = groups[v], groups[1 - v]
            wait_all(0, v, g_phase, lambda n, at: r_ref.at[v, at])
            gathered[v] = wide(r_ref, v, ng)
            places = [at_of(step) for step in steps] + [groups[1 - v][1]]
            for n in range(0, len(places), 2):
                for m, value in zip((n, n + 1), rows_of(v, places[n:n + 2])):
                    if m == len(steps):
                        own[v] = value
                        continue
                    p_send[v, m] = value.astype(bf16)
                    send(copy(1, v, phase, m, p_send.at[v, m], p_recv.at[v, m]))
        for v in (0, 1):
            wait_all(1, v, phase, lambda n, at: p_recv.at[v, n])
            total = own[v]
            for n in range(groups[1 - v][0] - 1):
                total = total + p_recv[v, n].astype(f32)
            use(v, total)

    firsts = []

    def use_first(v, total):
        ns, me, *_ = groups[1 - v]
        first = (STEP * total).astype(bf16)
        firsts.append(first.astype(f32))
        first_ref[v, me] = first
        for n in range(ns - 1):
            send(copy(1, v, 1, n, first_ref.at[v, me], first_ref.at[v, me]))

    scatter_gradient(0, 1, r1_ref, p1_send, p1_recv, use_first)
    fields = []

    def sums_of(v, pair):
        some = jnp.concatenate(
            [m_refs[v][:, pl.ds(pl.multiple_of(g * TILE, TILE), TILE)] for g in pair], axis=1
        )
        value = mm(fields[v], some)
        return value[:, :TILE], value[:, TILE:]

    sums = {}
    for v in (0, 1):
        (_, _, steps, at_of, _, _), (ns, *_) = groups[v], groups[1 - v]
        wait_all(1, v, 1, lambda n, at: first_ref.at[v, at])
        fields.append(wide(first_ref, v, ns))
        places = [at_of(step) for step in steps] + [groups[v][1]]
        for n in range(0, len(places), 2):
            for m, value in zip((n, n + 1), sums_of(v, places[n:n + 2])):
                if m == len(steps):
                    sums[v] = value
                    continue
                s_send[v, m] = value.astype(bf16)
                send(copy(0, v, 2, m, s_send.at[v, m], s_recv.at[v, m]))
    for v in (0, 1):
        wait_all(0, v, 2, lambda n, at: s_recv.at[v, n])
        for n in range(groups[v][0] - 1):
            sums[v] = sums[v] + s_recv[v, n].astype(f32)
    landed = jnp.zeros((TILE, 2 * TILE), f32)
    for half in split(jnp.concatenate([sums[0], sums[1]], axis=0).T):
        blank = jnp.zeros((TILES, TILE), bf16)
        masked = jnp.concatenate([
            jnp.concatenate([jnp.where(slots[p] == a, part(half, p), blank) for a in range(ANG)], axis=1)
            for p in range(PROJ)
        ], axis=0)
        landed = landed + mm(masked, weights)
    plane = landed[:, :TILE] + shift_down(landed[:, TILE:])
    plane_ref[...] = plane.astype(bf16)
    for step in SLAB_OFFS:
        send(z_copy(step), z_valid(step))
    for step in SLAB_OFFS:
        pl.when(z_valid(step))(z_arrival(step).wait_recv)
    planes = {step: planes_ref[z_index(step)].astype(f32) for step in SLAB_OFFS}
    planes[0] = plane
    seen = {-1: below, 0: measured, 1: above}

    def misfit_at(v):
        return jnp.concatenate([
            cone(0, v, p) * part(planes[v - 1], p) + cone(1, v, p) * part(planes[v], p)
            + cone(2, v, p) * part(planes[v + 1], p) - part(seen[v], p)
            for p in range(PROJ)
        ], axis=0)

    misfit = misfit_at(0)
    misfit_ref[...] = misfit

    send_responses(3, r2_ref, back_of(misfit_at(-1), misfit, misfit_at(1)))
    updates = []
    scatter_gradient(2, 3, r2_ref, p2_send, p2_recv, lambda v, total: updates.append(total))
    rows_now = jnp.concatenate(
        [first - STEP * update for first, update in zip(firsts, updates)], axis=0
    ).T.astype(bf16)
    coef_ref[...] = jnp.concatenate(
        [rows_now[i * BASIS:(i + 1) * BASIS] for i in range(TILES)], axis=1
    )

    finish()


def local(grid, slabs, measured, basis_time, frame_index, angle_slot, proj_weights, tile_offsets, cone_weights):
    ny, nz, nx = grid
    na, nb = nz, ny * nx
    most = max(na, nb)
    block, blocks = (TILE, TILE), (VIEWS, most, UC, TILE)
    vmem = pl.BlockSpec(memory_space=pltpu.VMEM)
    hbm = pl.BlockSpec(memory_space=pltpu.HBM)
    coefficients, misfit = pl.pallas_call(
        functools.partial(kernel, grid, slabs),
        out_shape=(
            pltpu.VMEM((BASIS, TILES * TILE), bf16),
            pltpu.VMEM(block, f32),
        ),
        in_specs=[hbm] * 7,
        out_specs=(vmem, vmem),
        scratch_shapes=[
            pltpu.VMEM(block, f32),
            pltpu.VMEM((BASIS, 32), f32),
            pltpu.SMEM((PROJ,), i32),
            pltpu.SMEM((PROJ,), i32),
            pltpu.VMEM((ANG, TILE, 2 * TILE), bf16),
            pltpu.VMEM((ANG, TILES, na * nb), i32),
            pltpu.SMEM((3, slabs, PROJ), f32),
            pltpu.SemaphoreType.DMA((7,)),
            pltpu.VMEM((VIEWS, most, 24, TILE), f32),
            pltpu.VMEM((VIEWS, most, 24, TILE), f32),
            pltpu.VMEM((VIEWS, TILES, na * nb, TILE), f32),
            pltpu.VMEM((VIEWS, PROJ, na * nb, TILE), f32),
            pltpu.VMEM((nb * TILE, na * TILE), bf16),
            pltpu.VMEM((na * TILE, nb * TILE), bf16),
            pltpu.VMEM((na * TILE, nb * TILE), bf16),
            pltpu.VMEM((nb * TILE, na * TILE), bf16),
            pltpu.VMEM(block, f32),
            pltpu.VMEM(block, bf16),
            pltpu.VMEM(block, bf16),
            pltpu.VMEM(block, bf16),
            pltpu.VMEM((4,) + block, bf16),
            pltpu.VMEM(blocks, bf16),
            pltpu.VMEM(blocks, bf16),
            pltpu.VMEM(blocks, bf16),
            pltpu.VMEM(blocks, bf16),
            pltpu.VMEM(blocks, bf16),
            pltpu.VMEM(blocks, bf16),
            pltpu.VMEM(blocks, bf16),
            pltpu.VMEM(blocks, bf16),
            pltpu.VMEM(blocks, bf16),
            pltpu.SemaphoreType.DMA((VIEWS, 4, most - 1)),
            pltpu.SemaphoreType.DMA((VIEWS, 4, most - 1)),
            pltpu.SemaphoreType.DMA((VIEWS, 3, most - 1)),
            pltpu.SemaphoreType.DMA((VIEWS, 3, most - 1)),
            pltpu.SemaphoreType.DMA((4,)),
            pltpu.SemaphoreType.DMA((4,)),
            pltpu.SemaphoreType.DMA((2,)),
            pltpu.SemaphoreType.DMA((2,)),
        ],
        compiler_params=pltpu.CompilerParams(
            collective_id=0, has_side_effects=True, vmem_limit_bytes=62 * 1000 * 1000
        ),
        name="two_gradients",
    )(
        measured.reshape(block),
        basis_time.T,
        frame_index,
        angle_slot,
        proj_weights,
        tile_offsets.transpose(0, 2, 1),
        cone_weights.transpose(0, 2, 1),
    )
    return (
        coefficients.reshape(1, BASIS, 1, TILES * TILE),
        misfit.reshape(PROJ, 1, TILES * TILE),
    )


def solution(mesh):
    placed = (
        P("angle", "zslab", None),
        P(),
        P("angle"),
        P("angle"),
        P("angle", None, None),
        P("angle", None, None),
        P(None, "angle", None),
    )
    grid = GRIDS[mesh.shape["angle"]]
    return jax.shard_map(
        functools.partial(local, grid, mesh.shape["zslab"]),
        mesh=mesh,
        in_specs=placed,
        out_specs=(P("angle", None, "zslab", None), P("angle", "zslab", None)),
        check_vma=False,
    )
```

```python
import functools

import jax
import jax.numpy as jnp
from jax import lax
from jax.experimental import pallas as pl
from jax.experimental.pallas import tpu as pltpu
from jax.sharding import PartitionSpec as P

GRIDS = {64: (4, 8, 2), 8: (2, 2, 2)}
MESH = pl.DeviceIdType.MESH
STEP = 0.4
TILE = 128
BASIS = 8
PROJ = 8
ANG = 4
TILES = 16
VIEWS = 2
UC = TILE // VIEWS
f32, bf16, i32 = jnp.float32, jnp.bfloat16, jnp.int32
SLAB_OFFS = (-2, 2, -1, 1)

NN = (((1,), (0,)), ((), ()))
NT = (((1,), (1,)), ((), ()))


def mm(a, b, dims=NN):
    return lax.dot_general(a, b, dims, preferred_element_type=f32)


def split(value):
    high = value.astype(bf16)
    return high, (value - high.astype(f32)).astype(bf16)


def iota(shape, dim):
    return lax.broadcasted_iota(i32, shape, dim)


def kernel(
    grid, slabs,
    meas_hbm, basis_hbm, frame_hbm, slot_hbm, w_hbm, off_hbm, cone_hbm,
    coef_ref, misfit_ref,
    meas_ref, basis_ref, frame_ref, slot_ref, w_ref, off_ref, cone_ref, load_sem,
    meta_send, meta_recv, x_ref, xt_ref, ma_ref, mb_ref, mta_ref, mtb_ref, near_ref, edge_ref, far_ref, plane_ref, planes_ref,
    r1_ref, r2_ref, p1_send, p1_recv, p2_send, p2_recv, first_ref, s_send, s_recv,
    g_ss, g_rs, c_ss, c_rs, z_ss, z_rs, h_ss, h_rs,
):
    ny, nz, nx = grid
    na, nb = nz, ny * nx
    slab = lax.axis_index("zslab")
    place = lax.axis_index("angle")
    my_x = place % nx
    alpha = (place // nx) % nz
    my_y = place // (nx * nz)
    beta = my_y * nx + my_x

    a_steps = sorted(range(1, na), key=lambda d: -min(d, na - d))
    b_steps = sorted(
        [(dy, dx) for dy in range(ny) for dx in range(nx) if dy or dx],
        key=lambda s: -(min(s[0], ny - s[0]) + s[1]),
    )

    def a_at(step):
        return lax.rem(alpha + step + na, na)

    def a_device(step):
        return my_y * (nz * nx) + a_at(step) * nx + my_x

    def b_at(step):
        return lax.rem(my_y + step[0] + ny, ny) * nx + lax.rem(my_x + step[1] + nx, nx)

    def b_device(step):
        other = b_at(step)
        return (other // nx) * (nz * nx) + alpha * nx + other % nx

    groups = (
        (na, alpha, a_steps, a_at, a_device, lambda step: -step),
        (nb, beta, b_steps, b_at, b_device, lambda step: (-step[0], -step[1])),
    )
    m_refs, mt_refs = (ma_ref, mb_ref), (mta_ref, mtb_ref)

    def copy(kind, v, phase, n, src, dst):
        _, _, steps, _, device, _ = groups[(v + kind) % 2]
        ss, rs = (g_ss, g_rs) if kind == 0 else (c_ss, c_rs)
        return pltpu.make_async_remote_copy(
            src_ref=src, dst_ref=dst, send_sem=ss.at[v, phase, n], recv_sem=rs.at[v, phase, n],
            device_id={"angle": device(steps[n])}, device_id_type=MESH,
        )

    def wait_all(kind, v, phase, ref_of):
        _, _, steps, at, _, opposite = groups[(v + kind) % 2]
        for n, step in enumerate(steps):
            ref = ref_of(n, at(opposite(step)))
            copy(kind, v, phase, n, ref, ref).wait_recv()

    def z_valid(step):
        return jnp.logical_and(slab + step >= 0, slab + step < slabs)

    def z_index(step):
        return SLAB_OFFS.index(step)

    def z_copy(step):
        back_slot = z_index(-step)
        return pltpu.make_async_remote_copy(
            src_ref=plane_ref, dst_ref=planes_ref.at[back_slot], send_sem=z_ss.at[z_index(step)],
            recv_sem=z_rs.at[back_slot], device_id={"zslab": slab + step}, device_id_type=MESH,
        )

    def z_arrival(step):
        slot = z_index(step)
        return pltpu.make_async_remote_copy(
            src_ref=plane_ref, dst_ref=planes_ref.at[slot], send_sem=z_ss.at[slot],
            recv_sem=z_rs.at[slot], device_id={"zslab": slab + step}, device_id_type=MESH,
        )

    odd = slab % 2
    near_copy = pltpu.make_async_remote_copy(
        src_ref=meas_ref, dst_ref=near_ref, send_sem=h_ss.at[0], recv_sem=h_rs.at[0],
        device_id={"zslab": slab + 1 - 2 * odd}, device_id_type=MESH,
    )
    far_step = 2 * odd - 1
    far_valid = jnp.logical_and(slab + far_step >= 0, slab + far_step < slabs)
    far_copy = pltpu.make_async_remote_copy(
        src_ref=edge_ref, dst_ref=far_ref, send_sem=h_ss.at[1], recv_sem=h_rs.at[1],
        device_id={"zslab": slab + far_step}, device_id_type=MESH,
    )

    loads = [
        pltpu.make_async_copy(source, target, load_sem.at[n])
        for n, (source, target) in enumerate([
            (slot_hbm, slot_ref), (off_hbm, off_ref), (frame_hbm, frame_ref), (basis_hbm, basis_ref),
            (meas_hbm, meas_ref), (cone_hbm, cone_ref), (w_hbm, w_ref),
        ])
    ]
    sent = []

    def send(copy, valid=None):
        if valid is None:
            copy.start()
        else:
            pl.when(valid)(copy.start)
        sent.append((copy, valid))

    def finish():
        for copy, valid in sent:
            if valid is None:
                copy.wait_send()
            else:
                pl.when(valid)(copy.wait_send)

    barrier = pltpu.get_barrier_semaphore()
    for step in sorted(range(1, slabs), key=lambda d: -min(d, slabs - d)):
        pl.semaphore_signal(
            barrier, inc=1, device_id={"zslab": lax.rem(slab + step, slabs)}, device_id_type=MESH
        )
    for step in a_steps:
        pl.semaphore_signal(barrier, inc=1, device_id={"angle": a_device(step)}, device_id_type=MESH)
    for step in b_steps:
        pl.semaphore_signal(barrier, inc=1, device_id={"angle": b_device(step)}, device_id_type=MESH)
    for load in loads:
        load.start()

    for load in loads[:4]:
        load.wait()
    slots = [slot_ref[p] for p in range(PROJ)]
    rows = iota((PROJ * TILES, ANG * TILES), 0)
    cols = iota((PROJ * TILES, ANG * TILES), 1)
    slot_rows = jnp.concatenate(
        [jnp.full((TILES, ANG * TILES), slots[p], i32) for p in range(PROJ)], axis=0
    )
    pick = jnp.logical_and((rows & (TILES - 1)) == (cols & (TILES - 1)), slot_rows == (cols >> 4))
    offs = off_ref[...].reshape(ANG * TILES, na * nb).astype(f32).astype(bf16)
    offs_p = mm(pick.astype(f32).astype(bf16), offs)
    offs_sent = []
    order = iota((na * nb, na * nb), 0)
    for o_alpha, o_beta in ((order // nb, order % nb), (order % na, order // na)):
        image_row = (o_beta // nx) * (nz * nx) + o_alpha * nx + o_beta % nx
        permute = (image_row == iota((na * nb, na * nb), 1)).astype(f32).astype(bf16)
        offs_sent.append(mm(permute, offs_p.astype(bf16), NT))

    lane_p = iota((32, TILE), 1) >> 4
    frames = jnp.zeros((32, TILE), i32)
    for p in range(PROJ):
        frames = jnp.where(lane_p == p, frame_ref[p], frames)
    hot = (frames == iota((32, TILE), 0)).astype(f32)
    phi = lax.dot_general(
        basis_ref[...], hot, NN, precision=lax.Precision.HIGHEST, preferred_element_type=f32
    )
    rows_p = iota((PROJ, 32), 0)
    frames = jnp.zeros((PROJ, 32), i32)
    for p in range(PROJ):
        frames = jnp.where(rows_p == p, frame_ref[p], frames)
    hot = (frames == iota((PROJ, 32), 1)).astype(f32)
    phi_rows = lax.dot_general(
        hot, jnp.concatenate([basis_ref[...]] * TILES, axis=0), NT,
        precision=lax.Precision.HIGHEST, preferred_element_type=f32,
    )
    for v in range(VIEWS):
        (ng, me, *_), (ns, *_) = groups[v], groups[1 - v]
        for g in range(ng):
            meta_send[v, g, 0:ns, :] = offs_sent[v][g * ns:(g + 1) * ns]
            meta_send[v, g, 8:16, :] = phi
            meta_send[v, g, 16:24, :] = phi_rows
        meta_recv[v, me] = meta_send[v, me]

    for step in SLAB_OFFS:
        @pl.when(jnp.logical_not(z_valid(step)))
        def _():
            planes_ref[z_index(step)] = jnp.zeros((TILE, TILE), bf16)

    @pl.when(jnp.logical_not(far_valid))
    def _():
        far_ref[...] = jnp.zeros((TILE, TILE), bf16)

    for load in loads[4:]:
        load.wait()
    edge_ref[...] = meas_ref[...].astype(bf16)
    pl.semaphore_wait(barrier, len(a_steps) + len(b_steps) + slabs - 1)

    send(far_copy, far_valid)
    send(near_copy)
    for v in range(VIEWS):
        _, me, steps, at, _, _ = groups[v]
        for n, step in enumerate(steps):
            send(copy(0, v, 0, n, meta_send.at[v, at(step)], meta_recv.at[v, me]))

    def cone(kind, step, p):
        at = jnp.clip(slab + step, 0, slabs - 1)
        return cone_ref[kind, at, p]

    def cone_masked(kind, step, p):
        return jnp.where(z_valid(step), cone(kind, step, p), 0.0)

    def part(value, p):
        return value[p * TILES:(p + 1) * TILES]

    def back_of(below, here, above):
        return jnp.concatenate([
            cone_masked(0, 1, p) * part(above, p) + cone(1, 0, p) * part(here, p)
            + cone_masked(2, -1, p) * part(below, p)
            for p in range(PROJ)
        ], axis=0)

    def shift_up(value):
        return jnp.concatenate([value[1:], value[:1]], axis=0)

    def shift_down(value):
        return jnp.concatenate([value[-1:], value[:-1]], axis=0)

    weights = w_ref[...].reshape(ANG * TILE, 2 * TILE)
    slot_lane = jnp.concatenate(
        [jnp.full((8, TILES), slots[p], i32) for p in range(PROJ)], axis=1
    )

    def send_responses(phase, r_ref, back):
        high, low = split(jnp.concatenate([back, shift_up(back)], axis=1))
        owner = jnp.broadcast_to(slot_lane[:1], (UC, TILE))
        for v in range(VIEWS):
            ng, me, *_ = groups[v]
            some = jnp.concatenate([w_ref[a, v * UC:(v + 1) * UC, :] for a in range(ANG)], axis=0)
            every = mm(some, high, NT) + mm(some, low, NT)
            own = jnp.zeros((UC, TILE), f32)
            for a in range(ANG):
                own = jnp.where(owner == a, every[a * UC:(a + 1) * UC], own)
            r_ref[v, me] = own.astype(bf16)
            for n in range(ng - 1):
                send(copy(0, v, phase, n, r_ref.at[v, me], r_ref.at[v, me]))

    near_copy.wait_recv()
    pl.when(far_valid)(far_copy.wait_recv)
    measured = meas_ref[...]
    beside, beyond = near_ref[...], far_ref[...].astype(f32)
    below = jnp.where(odd == 1, beside, beyond)
    above = jnp.where(odd == 1, beyond, beside)
    send_responses(1, r1_ref, back_of(below, measured, above))

    e_row, e_col = iota((TILE, TILE), 0), iota((TILE, TILE), 1)
    same = (e_row >> 4) == (e_col >> 4)
    tile_row = iota((TILES, TILE), 0).astype(f32)
    tile_lane = (iota((BASIS, TILE), 1) & (TILES - 1)).astype(f32)
    for v in (1, 0):
        (ng, *_), (ns, *_), m_ref = groups[v], groups[1 - v], m_refs[v]
        wait_all(0, v, 0, lambda n, at: meta_recv.at[v, at])
        near = jnp.concatenate([meta_recv[v, g, 0:ns, :] for g in range(ng)], axis=0).astype(bf16)
        for i in range(TILES):
            expand = jnp.logical_and(same, (e_row & (TILES - 1)) == i).astype(f32).astype(bf16)
            x_ref[v, i] = mm(near, expand)
        for p in range(PROJ):
            expand = jnp.logical_and(e_row >> 4 == p, (e_row & (TILES - 1)) == (e_col >> 3))
            xt_ref[v, p] = mm(near, expand.astype(f32).astype(bf16))
        factors = [meta_recv[v, g, 8:16, :] for g in range(ng)]

        def build(b, carry):
            for pair in range(TILES // 2):
                for g in range(ng):
                    lines = []
                    for i in (2 * pair, 2 * pair + 1):
                        line = x_ref[v, i, pl.ds(g * ns + b, 1), :]
                        hit = jnp.broadcast_to(line, (BASIS, TILE)) == tile_lane
                        lines.append(jnp.where(hit, factors[g], 0.0))
                    at = pl.ds(pl.multiple_of(b * TILE + pair * 16, 16), 16)
                    m_ref[at, g * TILE:(g + 1) * TILE] = jnp.concatenate(lines, axis=0).astype(bf16)
            at = pl.ds(pl.multiple_of(b * TILE, TILE), TILE)
            for g in range(ng):
                for p in range(PROJ):
                    line = xt_ref[v, p, pl.ds(g * ns + b, 1), :]
                    hit = jnp.broadcast_to(line, (TILES, TILE)) == tile_row
                    factor = jnp.broadcast_to(meta_recv[v, g, 16 + p:17 + p, :], (TILES, TILE))
                    mt_refs[v][g * TILE + p * TILES:g * TILE + (p + 1) * TILES, at] = jnp.where(
                        hit, factor, 0.0
                    ).astype(bf16)
            return carry

        lax.fori_loop(0, ns, build, 0)

    def wide(ref, c, count):
        return jnp.concatenate([ref[c, j] for j in range(count)], axis=1)

    def scatter_gradient(phase, g_phase, r_ref, p_send, p_recv, use):
        gathered = {}

        def rows_of(v, pair):
            some = jnp.concatenate(
                [mt_refs[v][:, pl.ds(pl.multiple_of(b * TILE, TILE), TILE)] for b in pair], axis=1
            )
            value = mm(gathered[v], some)
            return value[:, :TILE], value[:, TILE:]

        own = {}
        for v in (1, 0):
            (ng, *_), (_, _, steps, at_of, _, _) = groups[v], groups[1 - v]
            wait_all(0, v, g_phase, lambda n, at: r_ref.at[v, at])
            gathered[v] = wide(r_ref, v, ng)
            places = [at_of(step) for step in steps] + [groups[1 - v][1]]
            for n in range(0, len(places), 2):
                for m, value in zip((n, n + 1), rows_of(v, places[n:n + 2])):
                    if m == len(steps):
                        own[v] = value
                        continue
                    p_send[v, m] = value.astype(bf16)
                    send(copy(1, v, phase, m, p_send.at[v, m], p_recv.at[v, m]))
        for v in (1, 0):
            wait_all(1, v, phase, lambda n, at: p_recv.at[v, n])
            total = own[v]
            for n in range(groups[1 - v][0] - 1):
                total = total + p_recv[v, n].astype(f32)
            use(v, total)

    firsts = {}

    def use_first(v, total):
        ns, me, *_ = groups[1 - v]
        first = (STEP * total).astype(bf16)
        firsts[v] = first.astype(f32)
        first_ref[v, me] = first
        for n in range(ns - 1):
            send(copy(1, v, 1, n, first_ref.at[v, me], first_ref.at[v, me]))

    scatter_gradient(0, 1, r1_ref, p1_send, p1_recv, use_first)
    fields = []

    def sums_of(v, pair):
        some = jnp.concatenate(
            [m_refs[v][:, pl.ds(pl.multiple_of(g * TILE, TILE), TILE)] for g in pair], axis=1
        )
        value = mm(fields[v], some)
        return value[:, :TILE], value[:, TILE:]

    sums = {}
    for v in (0, 1):
        (_, _, steps, at_of, _, _), (ns, *_) = groups[v], groups[1 - v]
        wait_all(1, v, 1, lambda n, at: first_ref.at[v, at])
        fields.append(wide(first_ref, v, ns))
        places = [at_of(step) for step in steps] + [groups[v][1]]
        for n in range(0, len(places), 2):
            for m, value in zip((n, n + 1), sums_of(v, places[n:n + 2])):
                if m == len(steps):
                    sums[v] = value
                    continue
                s_send[v, m] = value.astype(bf16)
                send(copy(0, v, 2, m, s_send.at[v, m], s_recv.at[v, m]))
    for v in (0, 1):
        wait_all(0, v, 2, lambda n, at: s_recv.at[v, n])
        for n in range(groups[v][0] - 1):
            sums[v] = sums[v] + s_recv[v, n].astype(f32)
    landed = jnp.zeros((TILE, 2 * TILE), f32)
    for half in split(jnp.concatenate([sums[0], sums[1]], axis=0).T):
        blank = jnp.zeros((TILES, TILE), bf16)
        masked = jnp.concatenate([
            jnp.concatenate([jnp.where(slots[p] == a, part(half, p), blank) for a in range(ANG)], axis=1)
            for p in range(PROJ)
        ], axis=0)
        landed = landed + mm(masked, weights)
    plane = landed[:, :TILE] + shift_down(landed[:, TILE:])
    plane_ref[...] = plane.astype(bf16)
    for step in SLAB_OFFS:
        send(z_copy(step), z_valid(step))
    for step in SLAB_OFFS:
        pl.when(z_valid(step))(z_arrival(step).wait_recv)
    planes = {step: planes_ref[z_index(step)].astype(f32) for step in SLAB_OFFS}
    planes[0] = plane
    seen = {-1: below, 0: measured, 1: above}

    def misfit_at(v):
        return jnp.concatenate([
            cone(0, v, p) * part(planes[v - 1], p) + cone(1, v, p) * part(planes[v], p)
            + cone(2, v, p) * part(planes[v + 1], p) - part(seen[v], p)
            for p in range(PROJ)
        ], axis=0)

    misfit = misfit_at(0)
    misfit_ref[...] = misfit

    send_responses(3, r2_ref, back_of(misfit_at(-1), misfit, misfit_at(1)))
    updates = {}
    scatter_gradient(2, 3, r2_ref, p2_send, p2_recv, updates.__setitem__)
    rows_now = jnp.concatenate(
        [firsts[v] - STEP * updates[v] for v in range(VIEWS)], axis=0
    ).T.astype(bf16)
    coef_ref[...] = jnp.concatenate(
        [rows_now[i * BASIS:(i + 1) * BASIS] for i in range(TILES)], axis=1
    )

    finish()


def local(grid, slabs, measured, basis_time, frame_index, angle_slot, proj_weights, tile_offsets, cone_weights):
    ny, nz, nx = grid
    na, nb = nz, ny * nx
    most = max(na, nb)
    block, blocks = (TILE, TILE), (VIEWS, most, UC, TILE)
    vmem = pl.BlockSpec(memory_space=pltpu.VMEM)
    hbm = pl.BlockSpec(memory_space=pltpu.HBM)
    coefficients, misfit = pl.pallas_call(
        functools.partial(kernel, grid, slabs),
        out_shape=(
            pltpu.VMEM((BASIS, TILES * TILE), bf16),
            pltpu.VMEM(block, f32),
        ),
        in_specs=[hbm] * 7,
        out_specs=(vmem, vmem),
        scratch_shapes=[
            pltpu.VMEM(block, f32),
            pltpu.VMEM((BASIS, 32), f32),
            pltpu.SMEM((PROJ,), i32),
            pltpu.SMEM((PROJ,), i32),
            pltpu.VMEM((ANG, TILE, 2 * TILE), bf16),
            pltpu.VMEM((ANG, TILES, na * nb), i32),
            pltpu.SMEM((3, slabs, PROJ), f32),
            pltpu.SemaphoreType.DMA((7,)),
            pltpu.VMEM((VIEWS, most, 24, TILE), f32),
            pltpu.VMEM((VIEWS, most, 24, TILE), f32),
            pltpu.VMEM((VIEWS, TILES, na * nb, TILE), f32),
            pltpu.VMEM((VIEWS, PROJ, na * nb, TILE), f32),
            pltpu.VMEM((nb * TILE, na * TILE), bf16),
            pltpu.VMEM((na * TILE, nb * TILE), bf16),
            pltpu.VMEM((na * TILE, nb * TILE), bf16),
            pltpu.VMEM((nb * TILE, na * TILE), bf16),
            pltpu.VMEM(block, f32),
            pltpu.VMEM(block, bf16),
            pltpu.VMEM(block, bf16),
            pltpu.VMEM(block, bf16),
            pltpu.VMEM((4,) + block, bf16),
            pltpu.VMEM(blocks, bf16),
            pltpu.VMEM(blocks, bf16),
            pltpu.VMEM(blocks, bf16),
            pltpu.VMEM(blocks, bf16),
            pltpu.VMEM(blocks, bf16),
            pltpu.VMEM(blocks, bf16),
            pltpu.VMEM(blocks, bf16),
            pltpu.VMEM(blocks, bf16),
            pltpu.VMEM(blocks, bf16),
            pltpu.SemaphoreType.DMA((VIEWS, 4, most - 1)),
            pltpu.SemaphoreType.DMA((VIEWS, 4, most - 1)),
            pltpu.SemaphoreType.DMA((VIEWS, 3, most - 1)),
            pltpu.SemaphoreType.DMA((VIEWS, 3, most - 1)),
            pltpu.SemaphoreType.DMA((4,)),
            pltpu.SemaphoreType.DMA((4,)),
            pltpu.SemaphoreType.DMA((2,)),
            pltpu.SemaphoreType.DMA((2,)),
        ],
        compiler_params=pltpu.CompilerParams(
            collective_id=0, has_side_effects=True, vmem_limit_bytes=62 * 1000 * 1000
        ),
        name="two_gradients",
    )(
        measured.reshape(block),
        basis_time.T,
        frame_index,
        angle_slot,
        proj_weights,
        tile_offsets.transpose(0, 2, 1),
        cone_weights.transpose(0, 2, 1),
    )
    return (
        coefficients.reshape(1, BASIS, 1, TILES * TILE),
        misfit.reshape(PROJ, 1, TILES * TILE),
    )


def solution(mesh):
    placed = (
        P("angle", "zslab", None),
        P(),
        P("angle"),
        P("angle"),
        P("angle", None, None),
        P("angle", None, None),
        P(None, "angle", None),
    )
    grid = GRIDS[mesh.shape["angle"]]
    return jax.shard_map(
        functools.partial(local, grid, mesh.shape["zslab"]),
        mesh=mesh,
        in_specs=placed,
        out_specs=(P("angle", None, "zslab", None), P("angle", "zslab", None)),
        check_vma=False,
    )
```

```python
import functools

import jax
import jax.numpy as jnp
from jax import lax
from jax.experimental import pallas as pl
from jax.experimental.pallas import tpu as pltpu
from jax.sharding import PartitionSpec as P

GRIDS = {64: (4, 8, 2), 8: (2, 2, 2)}
MESH = pl.DeviceIdType.MESH
STEP = 0.4
TILE = 128
BASIS = 8
PROJ = 8
ANG = 4
TILES = 16
VIEWS = 2
UC = TILE // VIEWS
f32, bf16, i32 = jnp.float32, jnp.bfloat16, jnp.int32
SLAB_OFFS = (-2, 2, -1, 1)

NN = (((1,), (0,)), ((), ()))
NT = (((1,), (1,)), ((), ()))


def mm(a, b, dims=NN):
    return lax.dot_general(a, b, dims, preferred_element_type=f32)


def split(value):
    high = value.astype(bf16)
    return high, (value - high.astype(f32)).astype(bf16)


def iota(shape, dim):
    return lax.broadcasted_iota(i32, shape, dim)


def kernel(
    grid, slabs,
    meas_hbm, basis_hbm, frame_hbm, slot_hbm, w_hbm, off_hbm, cone_hbm,
    coef_ref, misfit_ref,
    meas_ref, basis_ref, frame_ref, slot_ref, w_ref, off_ref, cone_ref, load_sem,
    meta_send, meta_recv, x_ref, xt_ref, ma_ref, mb_ref, mta_ref, mtb_ref, near_ref, edge_ref, far_ref, plane_ref, planes_ref,
    r1_ref, r2_ref, p1_send, p1_recv, p2_send, p2_recv, first_ref, s_send, s_recv,
    g_ss, g_rs, c_ss, c_rs, z_ss, z_rs, h_ss, h_rs,
):
    ny, nz, nx = grid
    na, nb = nz, ny * nx
    slab = lax.axis_index("zslab")
    place = lax.axis_index("angle")
    my_x = place % nx
    alpha = (place // nx) % nz
    my_y = place // (nx * nz)
    beta = my_y * nx + my_x

    a_steps = sorted(range(1, na), key=lambda d: -min(d, na - d))
    b_steps = sorted(
        [(dy, dx) for dy in range(ny) for dx in range(nx) if dy or dx],
        key=lambda s: -(min(s[0], ny - s[0]) + s[1]),
    )

    def a_at(step):
        return lax.rem(alpha + step + na, na)

    def a_device(step):
        return my_y * (nz * nx) + a_at(step) * nx + my_x

    def b_at(step):
        return lax.rem(my_y + step[0] + ny, ny) * nx + lax.rem(my_x + step[1] + nx, nx)

    def b_device(step):
        other = b_at(step)
        return (other // nx) * (nz * nx) + alpha * nx + other % nx

    groups = (
        (na, alpha, a_steps, a_at, a_device, lambda step: -step),
        (nb, beta, b_steps, b_at, b_device, lambda step: (-step[0], -step[1])),
    )
    m_refs, mt_refs = (ma_ref, mb_ref), (mta_ref, mtb_ref)

    def copy(kind, v, phase, n, src, dst):
        _, _, steps, _, device, _ = groups[(v + kind) % 2]
        ss, rs = (g_ss, g_rs) if kind == 0 else (c_ss, c_rs)
        return pltpu.make_async_remote_copy(
            src_ref=src, dst_ref=dst, send_sem=ss.at[v, phase, n], recv_sem=rs.at[v, phase, n],
            device_id={"angle": device(steps[n])}, device_id_type=MESH,
        )

    def wait_all(kind, v, phase, ref_of):
        _, _, steps, at, _, opposite = groups[(v + kind) % 2]
        for n, step in enumerate(steps):
            ref = ref_of(n, at(opposite(step)))
            copy(kind, v, phase, n, ref, ref).wait_recv()

    def z_valid(step):
        return jnp.logical_and(slab + step >= 0, slab + step < slabs)

    def z_index(step):
        return SLAB_OFFS.index(step)

    def z_copy(step):
        back_slot = z_index(-step)
        return pltpu.make_async_remote_copy(
            src_ref=plane_ref, dst_ref=planes_ref.at[back_slot], send_sem=z_ss.at[z_index(step)],
            recv_sem=z_rs.at[back_slot], device_id={"zslab": slab + step}, device_id_type=MESH,
        )

    def z_arrival(step):
        slot = z_index(step)
        return pltpu.make_async_remote_copy(
            src_ref=plane_ref, dst_ref=planes_ref.at[slot], send_sem=z_ss.at[slot],
            recv_sem=z_rs.at[slot], device_id={"zslab": slab + step}, device_id_type=MESH,
        )

    odd = slab % 2
    near_copy = pltpu.make_async_remote_copy(
        src_ref=meas_ref, dst_ref=near_ref, send_sem=h_ss.at[0], recv_sem=h_rs.at[0],
        device_id={"zslab": slab + 1 - 2 * odd}, device_id_type=MESH,
    )
    far_step = 2 * odd - 1
    far_valid = jnp.logical_and(slab + far_step >= 0, slab + far_step < slabs)
    far_copy = pltpu.make_async_remote_copy(
        src_ref=edge_ref, dst_ref=far_ref, send_sem=h_ss.at[1], recv_sem=h_rs.at[1],
        device_id={"zslab": slab + far_step}, device_id_type=MESH,
    )

    loads = [
        pltpu.make_async_copy(source, target, load_sem.at[n])
        for n, (source, target) in enumerate([
            (slot_hbm, slot_ref), (off_hbm, off_ref), (frame_hbm, frame_ref), (basis_hbm, basis_ref),
            (meas_hbm, meas_ref), (cone_hbm, cone_ref), (w_hbm, w_ref),
        ])
    ]
    sent = []

    def send(copy, valid=None):
        if valid is None:
            copy.start()
        else:
            pl.when(valid)(copy.start)
        sent.append((copy, valid))

    def finish():
        for copy, valid in sent:
            if valid is None:
                copy.wait_send()
            else:
                pl.when(valid)(copy.wait_send)

    barrier = pltpu.get_barrier_semaphore()
    for step in sorted(range(1, slabs), key=lambda d: -min(d, slabs - d)):
        pl.semaphore_signal(
            barrier, inc=1, device_id={"zslab": lax.rem(slab + step, slabs)}, device_id_type=MESH
        )
    for step in a_steps:
        pl.semaphore_signal(barrier, inc=1, device_id={"angle": a_device(step)}, device_id_type=MESH)
    for step in b_steps:
        pl.semaphore_signal(barrier, inc=1, device_id={"angle": b_device(step)}, device_id_type=MESH)
    for load in loads:
        load.start()

    for load in loads[:4]:
        load.wait()
    slots = [slot_ref[p] for p in range(PROJ)]
    rows = iota((PROJ * TILES, ANG * TILES), 0)
    cols = iota((PROJ * TILES, ANG * TILES), 1)
    slot_rows = jnp.concatenate(
        [jnp.full((TILES, ANG * TILES), slots[p], i32) for p in range(PROJ)], axis=0
    )
    pick = jnp.logical_and((rows & (TILES - 1)) == (cols & (TILES - 1)), slot_rows == (cols >> 4))
    offs = off_ref[...].reshape(ANG * TILES, na * nb).astype(f32).astype(bf16)
    offs_p = mm(pick.astype(f32).astype(bf16), offs)
    offs_sent = []
    order = iota((na * nb, na * nb), 0)
    for o_alpha, o_beta in ((order // nb, order % nb), (order % na, order // na)):
        image_row = (o_beta // nx) * (nz * nx) + o_alpha * nx + o_beta % nx
        permute = (image_row == iota((na * nb, na * nb), 1)).astype(f32).astype(bf16)
        offs_sent.append(mm(permute, offs_p.astype(bf16), NT))

    lane_p = iota((32, TILE), 1) >> 4
    frames = jnp.zeros((32, TILE), i32)
    for p in range(PROJ):
        frames = jnp.where(lane_p == p, frame_ref[p], frames)
    hot = (frames == iota((32, TILE), 0)).astype(f32)
    phi = lax.dot_general(
        basis_ref[...], hot, NN, precision=lax.Precision.HIGHEST, preferred_element_type=f32
    )
    rows_p = iota((PROJ, 32), 0)
    frames = jnp.zeros((PROJ, 32), i32)
    for p in range(PROJ):
        frames = jnp.where(rows_p == p, frame_ref[p], frames)
    hot = (frames == iota((PROJ, 32), 1)).astype(f32)
    phi_rows = lax.dot_general(
        hot, jnp.concatenate([basis_ref[...]] * TILES, axis=0), NT,
        precision=lax.Precision.HIGHEST, preferred_element_type=f32,
    )
    for v in range(VIEWS):
        (ng, me, *_), (ns, *_) = groups[v], groups[1 - v]
        for g in range(ng):
            meta_send[v, g, 0:ns, :] = offs_sent[v][g * ns:(g + 1) * ns]
            meta_send[v, g, 8:16, :] = phi
            meta_send[v, g, 16:24, :] = phi_rows
        meta_recv[v, me] = meta_send[v, me]

    for step in SLAB_OFFS:
        @pl.when(jnp.logical_not(z_valid(step)))
        def _():
            planes_ref[z_index(step)] = jnp.zeros((TILE, TILE), bf16)

    @pl.when(jnp.logical_not(far_valid))
    def _():
        far_ref[...] = jnp.zeros((TILE, TILE), bf16)

    for load in loads[4:]:
        load.wait()
    edge_ref[...] = meas_ref[...].astype(bf16)
    pl.semaphore_wait(barrier, len(a_steps) + len(b_steps) + slabs - 1)

    send(far_copy, far_valid)
    send(near_copy)
    for v in range(VIEWS):
        _, me, steps, at, _, _ = groups[v]
        for n, step in enumerate(steps):
            send(copy(0, v, 0, n, meta_send.at[v, at(step)], meta_recv.at[v, me]))

    def cone(kind, step, p):
        at = jnp.clip(slab + step, 0, slabs - 1)
        return cone_ref[kind, at, p]

    def cone_masked(kind, step, p):
        return jnp.where(z_valid(step), cone(kind, step, p), 0.0)

    def part(value, p):
        return value[p * TILES:(p + 1) * TILES]

    def back_of(below, here, above):
        return jnp.concatenate([
            cone_masked(0, 1, p) * part(above, p) + cone(1, 0, p) * part(here, p)
            + cone_masked(2, -1, p) * part(below, p)
            for p in range(PROJ)
        ], axis=0)

    def shift_up(value):
        return jnp.concatenate([value[1:], value[:1]], axis=0)

    def shift_down(value):
        return jnp.concatenate([value[-1:], value[:-1]], axis=0)

    weights = w_ref[...].reshape(ANG * TILE, 2 * TILE)
    slot_lane = jnp.concatenate(
        [jnp.full((8, TILES), slots[p], i32) for p in range(PROJ)], axis=1
    )

    def send_responses(phase, r_ref, back):
        high, low = split(jnp.concatenate([back, shift_up(back)], axis=1))
        owner = jnp.broadcast_to(slot_lane[:1], (UC, TILE))
        for v in range(VIEWS):
            ng, me, *_ = groups[v]
            some = jnp.concatenate([w_ref[a, v * UC:(v + 1) * UC, :] for a in range(ANG)], axis=0)
            every = mm(some, high, NT) + mm(some, low, NT)
            own = jnp.zeros((UC, TILE), f32)
            for a in range(ANG):
                own = jnp.where(owner == a, every[a * UC:(a + 1) * UC], own)
            r_ref[v, me] = own.astype(bf16)
            for n in range(ng - 1):
                send(copy(0, v, phase, n, r_ref.at[v, me], r_ref.at[v, me]))

    near_copy.wait_recv()
    pl.when(far_valid)(far_copy.wait_recv)
    measured = meas_ref[...]
    beside, beyond = near_ref[...], far_ref[...].astype(f32)
    below = jnp.where(odd == 1, beside, beyond)
    above = jnp.where(odd == 1, beyond, beside)
    send_responses(1, r1_ref, back_of(below, measured, above))

    e_row, e_col = iota((TILE, TILE), 0), iota((TILE, TILE), 1)
    same = (e_row >> 4) == (e_col >> 4)
    tile_row = iota((TILES, TILE), 0).astype(f32)
    tile_lane = (iota((BASIS, TILE), 1) & (TILES - 1)).astype(f32)
    def near_of(v):
        (ng, *_), (ns, *_) = groups[v], groups[1 - v]
        near = jnp.concatenate([meta_recv[v, g, 0:ns, :] for g in range(ng)], axis=0).astype(bf16)
        return ng, ns, near

    for v in (1, 0):
        wait_all(0, v, 0, lambda n, at: meta_recv.at[v, at])
        ng, ns, near = near_of(v)
        for p in range(PROJ):
            expand = jnp.logical_and(e_row >> 4 == p, (e_row & (TILES - 1)) == (e_col >> 3))
            xt_ref[v, p] = mm(near, expand.astype(f32).astype(bf16))

        def build_transposed(b, carry):
            at = pl.ds(pl.multiple_of(b * TILE, TILE), TILE)
            for g in range(ng):
                for p in range(PROJ):
                    line = xt_ref[v, p, pl.ds(g * ns + b, 1), :]
                    hit = jnp.broadcast_to(line, (TILES, TILE)) == tile_row
                    factor = jnp.broadcast_to(meta_recv[v, g, 16 + p:17 + p, :], (TILES, TILE))
                    mt_refs[v][g * TILE + p * TILES:g * TILE + (p + 1) * TILES, at] = jnp.where(
                        hit, factor, 0.0
                    ).astype(bf16)
            return carry

        lax.fori_loop(0, ns, build_transposed, 0)

    def build_plain():
        for v in (0, 1):
            ng, ns, near = near_of(v)
            for i in range(TILES):
                expand = jnp.logical_and(same, (e_row & (TILES - 1)) == i).astype(f32).astype(bf16)
                x_ref[v, i] = mm(near, expand)
            factors = [meta_recv[v, g, 8:16, :] for g in range(ng)]

            def build(b, carry):
                for pair in range(TILES // 2):
                    for g in range(ng):
                        lines = []
                        for i in (2 * pair, 2 * pair + 1):
                            line = x_ref[v, i, pl.ds(g * ns + b, 1), :]
                            hit = jnp.broadcast_to(line, (BASIS, TILE)) == tile_lane
                            lines.append(jnp.where(hit, factors[g], 0.0))
                        at = pl.ds(pl.multiple_of(b * TILE + pair * 16, 16), 16)
                        m_refs[v][at, g * TILE:(g + 1) * TILE] = jnp.concatenate(
                            lines, axis=0
                        ).astype(bf16)
                return carry

            lax.fori_loop(0, ns, build, 0)

    def wide(ref, c, count):
        return jnp.concatenate([ref[c, j] for j in range(count)], axis=1)

    def scatter_gradient(phase, g_phase, r_ref, p_send, p_recv, use, meanwhile=lambda: None):
        gathered = {}

        def rows_of(v, pair):
            some = jnp.concatenate(
                [mt_refs[v][:, pl.ds(pl.multiple_of(b * TILE, TILE), TILE)] for b in pair], axis=1
            )
            value = mm(gathered[v], some)
            return value[:, :TILE], value[:, TILE:]

        own = {}
        for v in (1, 0):
            (ng, *_), (_, _, steps, at_of, _, _) = groups[v], groups[1 - v]
            wait_all(0, v, g_phase, lambda n, at: r_ref.at[v, at])
            gathered[v] = wide(r_ref, v, ng)
            places = [at_of(step) for step in steps] + [groups[1 - v][1]]
            for n in range(0, len(places), 2):
                for m, value in zip((n, n + 1), rows_of(v, places[n:n + 2])):
                    if m == len(steps):
                        own[v] = value
                        continue
                    p_send[v, m] = value.astype(bf16)
                    send(copy(1, v, phase, m, p_send.at[v, m], p_recv.at[v, m]))
        meanwhile()
        for v in (1, 0):
            wait_all(1, v, phase, lambda n, at: p_recv.at[v, n])
            total = own[v]
            for n in range(groups[1 - v][0] - 1):
                total = total + p_recv[v, n].astype(f32)
            use(v, total)

    firsts = {}

    def use_first(v, total):
        ns, me, *_ = groups[1 - v]
        first = (STEP * total).astype(bf16)
        firsts[v] = first.astype(f32)
        first_ref[v, me] = first
        for n in range(ns - 1):
            send(copy(1, v, 1, n, first_ref.at[v, me], first_ref.at[v, me]))

    scatter_gradient(0, 1, r1_ref, p1_send, p1_recv, use_first, build_plain)
    fields = []

    def sums_of(v, pair):
        some = jnp.concatenate(
            [m_refs[v][:, pl.ds(pl.multiple_of(g * TILE, TILE), TILE)] for g in pair], axis=1
        )
        value = mm(fields[v], some)
        return value[:, :TILE], value[:, TILE:]

    sums = {}
    for v in (0, 1):
        (_, _, steps, at_of, _, _), (ns, *_) = groups[v], groups[1 - v]
        wait_all(1, v, 1, lambda n, at: first_ref.at[v, at])
        fields.append(wide(first_ref, v, ns))
        places = [at_of(step) for step in steps] + [groups[v][1]]
        for n in range(0, len(places), 2):
            for m, value in zip((n, n + 1), sums_of(v, places[n:n + 2])):
                if m == len(steps):
                    sums[v] = value
                    continue
                s_send[v, m] = value.astype(bf16)
                send(copy(0, v, 2, m, s_send.at[v, m], s_recv.at[v, m]))
    for v in (0, 1):
        wait_all(0, v, 2, lambda n, at: s_recv.at[v, n])
        for n in range(groups[v][0] - 1):
            sums[v] = sums[v] + s_recv[v, n].astype(f32)
    landed = jnp.zeros((TILE, 2 * TILE), f32)
    for half in split(jnp.concatenate([sums[0], sums[1]], axis=0).T):
        blank = jnp.zeros((TILES, TILE), bf16)
        masked = jnp.concatenate([
            jnp.concatenate([jnp.where(slots[p] == a, part(half, p), blank) for a in range(ANG)], axis=1)
            for p in range(PROJ)
        ], axis=0)
        landed = landed + mm(masked, weights)
    plane = landed[:, :TILE] + shift_down(landed[:, TILE:])
    plane_ref[...] = plane.astype(bf16)
    for step in SLAB_OFFS:
        send(z_copy(step), z_valid(step))
    for step in SLAB_OFFS:
        pl.when(z_valid(step))(z_arrival(step).wait_recv)
    planes = {step: planes_ref[z_index(step)].astype(f32) for step in SLAB_OFFS}
    planes[0] = plane
    seen = {-1: below, 0: measured, 1: above}

    def misfit_at(v):
        return jnp.concatenate([
            cone(0, v, p) * part(planes[v - 1], p) + cone(1, v, p) * part(planes[v], p)
            + cone(2, v, p) * part(planes[v + 1], p) - part(seen[v], p)
            for p in range(PROJ)
        ], axis=0)

    misfit = misfit_at(0)
    misfit_ref[...] = misfit

    send_responses(3, r2_ref, back_of(misfit_at(-1), misfit, misfit_at(1)))
    updates = {}
    scatter_gradient(2, 3, r2_ref, p2_send, p2_recv, updates.__setitem__)
    rows_now = jnp.concatenate(
        [firsts[v] - STEP * updates[v] for v in range(VIEWS)], axis=0
    ).T.astype(bf16)
    coef_ref[...] = jnp.concatenate(
        [rows_now[i * BASIS:(i + 1) * BASIS] for i in range(TILES)], axis=1
    )

    finish()


def local(grid, slabs, measured, basis_time, frame_index, angle_slot, proj_weights, tile_offsets, cone_weights):
    ny, nz, nx = grid
    na, nb = nz, ny * nx
    most = max(na, nb)
    block, blocks = (TILE, TILE), (VIEWS, most, UC, TILE)
    vmem = pl.BlockSpec(memory_space=pltpu.VMEM)
    hbm = pl.BlockSpec(memory_space=pltpu.HBM)
    coefficients, misfit = pl.pallas_call(
        functools.partial(kernel, grid, slabs),
        out_shape=(
            pltpu.VMEM((BASIS, TILES * TILE), bf16),
            pltpu.VMEM(block, f32),
        ),
        in_specs=[hbm] * 7,
        out_specs=(vmem, vmem),
        scratch_shapes=[
            pltpu.VMEM(block, f32),
            pltpu.VMEM((BASIS, 32), f32),
            pltpu.SMEM((PROJ,), i32),
            pltpu.SMEM((PROJ,), i32),
            pltpu.VMEM((ANG, TILE, 2 * TILE), bf16),
            pltpu.VMEM((ANG, TILES, na * nb), i32),
            pltpu.SMEM((3, slabs, PROJ), f32),
            pltpu.SemaphoreType.DMA((7,)),
            pltpu.VMEM((VIEWS, most, 24, TILE), f32),
            pltpu.VMEM((VIEWS, most, 24, TILE), f32),
            pltpu.VMEM((VIEWS, TILES, na * nb, TILE), f32),
            pltpu.VMEM((VIEWS, PROJ, na * nb, TILE), f32),
            pltpu.VMEM((nb * TILE, na * TILE), bf16),
            pltpu.VMEM((na * TILE, nb * TILE), bf16),
            pltpu.VMEM((na * TILE, nb * TILE), bf16),
            pltpu.VMEM((nb * TILE, na * TILE), bf16),
            pltpu.VMEM(block, f32),
            pltpu.VMEM(block, bf16),
            pltpu.VMEM(block, bf16),
            pltpu.VMEM(block, bf16),
            pltpu.VMEM((4,) + block, bf16),
            pltpu.VMEM(blocks, bf16),
            pltpu.VMEM(blocks, bf16),
            pltpu.VMEM(blocks, bf16),
            pltpu.VMEM(blocks, bf16),
            pltpu.VMEM(blocks, bf16),
            pltpu.VMEM(blocks, bf16),
            pltpu.VMEM(blocks, bf16),
            pltpu.VMEM(blocks, bf16),
            pltpu.VMEM(blocks, bf16),
            pltpu.SemaphoreType.DMA((VIEWS, 4, most - 1)),
            pltpu.SemaphoreType.DMA((VIEWS, 4, most - 1)),
            pltpu.SemaphoreType.DMA((VIEWS, 3, most - 1)),
            pltpu.SemaphoreType.DMA((VIEWS, 3, most - 1)),
            pltpu.SemaphoreType.DMA((4,)),
            pltpu.SemaphoreType.DMA((4,)),
            pltpu.SemaphoreType.DMA((2,)),
            pltpu.SemaphoreType.DMA((2,)),
        ],
        compiler_params=pltpu.CompilerParams(
            collective_id=0, has_side_effects=True, vmem_limit_bytes=62 * 1000 * 1000
        ),
        name="two_gradients",
    )(
        measured.reshape(block),
        basis_time.T,
        frame_index,
        angle_slot,
        proj_weights,
        tile_offsets.transpose(0, 2, 1),
        cone_weights.transpose(0, 2, 1),
    )
    return (
        coefficients.reshape(1, BASIS, 1, TILES * TILE),
        misfit.reshape(PROJ, 1, TILES * TILE),
    )


def solution(mesh):
    placed = (
        P("angle", "zslab", None),
        P(),
        P("angle"),
        P("angle"),
        P("angle", None, None),
        P("angle", None, None),
        P(None, "angle", None),
    )
    grid = GRIDS[mesh.shape["angle"]]
    return jax.shard_map(
        functools.partial(local, grid, mesh.shape["zslab"]),
        mesh=mesh,
        in_specs=placed,
        out_specs=(P("angle", None, "zslab", None), P("angle", "zslab", None)),
        check_vma=False,
    )
```

```python
import functools

import jax
import jax.numpy as jnp
from jax import lax
from jax.experimental import pallas as pl
from jax.experimental.pallas import tpu as pltpu
from jax.sharding import PartitionSpec as P

GRIDS = {64: (4, 8, 2), 8: (2, 2, 2)}
MESH = pl.DeviceIdType.MESH
STEP = 0.4
TILE = 128
BASIS = 8
PROJ = 8
ANG = 4
TILES = 16
VIEWS = 2
UC = TILE // VIEWS
f32, bf16, i32 = jnp.float32, jnp.bfloat16, jnp.int32
SLAB_OFFS = (-2, 2, -1, 1)

NN = (((1,), (0,)), ((), ()))
NT = (((1,), (1,)), ((), ()))


def mm(a, b, dims=NN):
    return lax.dot_general(a, b, dims, preferred_element_type=f32)


def split(value):
    high = value.astype(bf16)
    return high, (value - high.astype(f32)).astype(bf16)


def iota(shape, dim):
    return lax.broadcasted_iota(i32, shape, dim)


def kernel(
    grid, slabs,
    meas_hbm, basis_hbm, frame_hbm, slot_hbm, w_hbm, off_hbm, cone_hbm,
    coef_ref, misfit_ref,
    meas_ref, basis_ref, frame_ref, slot_ref, w_ref, off_ref, cone_ref, load_sem,
    meta_send, meta_recv, x_ref, xt_ref, ma_ref, mb_ref, mta_ref, mtb_ref, near_ref, edge_ref, far_ref, plane_ref, planes_ref,
    r1_ref, r2_ref, p1_send, p1_recv, p2_send, p2_recv, first_ref, s_send, s_recv,
    g_ss, g_rs, c_ss, c_rs, z_ss, z_rs, h_ss, h_rs,
):
    ny, nz, nx = grid
    na, nb = nz, ny * nx
    slab = lax.axis_index("zslab")
    place = lax.axis_index("angle")
    my_x = place % nx
    alpha = (place // nx) % nz
    my_y = place // (nx * nz)
    beta = my_y * nx + my_x

    a_steps = sorted(range(1, na), key=lambda d: -min(d, na - d))
    b_steps = sorted(
        [(dy, dx) for dy in range(ny) for dx in range(nx) if dy or dx],
        key=lambda s: -(min(s[0], ny - s[0]) + s[1]),
    )

    def a_at(step):
        return lax.rem(alpha + step + na, na)

    def a_device(step):
        return my_y * (nz * nx) + a_at(step) * nx + my_x

    def b_at(step):
        return lax.rem(my_y + step[0] + ny, ny) * nx + lax.rem(my_x + step[1] + nx, nx)

    def b_device(step):
        other = b_at(step)
        return (other // nx) * (nz * nx) + alpha * nx + other % nx

    groups = (
        (na, alpha, a_steps, a_at, a_device, lambda step: -step),
        (nb, beta, b_steps, b_at, b_device, lambda step: (-step[0], -step[1])),
    )
    m_refs, mt_refs = (ma_ref, mb_ref), (mta_ref, mtb_ref)

    def copy(kind, v, phase, n, src, dst):
        _, _, steps, _, device, _ = groups[(v + kind) % 2]
        ss, rs = (g_ss, g_rs) if kind == 0 else (c_ss, c_rs)
        return pltpu.make_async_remote_copy(
            src_ref=src, dst_ref=dst, send_sem=ss.at[v, phase, n], recv_sem=rs.at[v, phase, n],
            device_id={"angle": device(steps[n])}, device_id_type=MESH,
        )

    def wait_all(kind, v, phase, ref_of):
        _, _, steps, at, _, opposite = groups[(v + kind) % 2]
        for n, step in enumerate(steps):
            ref = ref_of(n, at(opposite(step)))
            copy(kind, v, phase, n, ref, ref).wait_recv()

    def z_valid(step):
        return jnp.logical_and(slab + step >= 0, slab + step < slabs)

    def z_index(step):
        return SLAB_OFFS.index(step)

    def z_copy(step):
        back_slot = z_index(-step)
        return pltpu.make_async_remote_copy(
            src_ref=plane_ref, dst_ref=planes_ref.at[back_slot], send_sem=z_ss.at[z_index(step)],
            recv_sem=z_rs.at[back_slot], device_id={"zslab": slab + step}, device_id_type=MESH,
        )

    def z_arrival(step):
        slot = z_index(step)
        return pltpu.make_async_remote_copy(
            src_ref=plane_ref, dst_ref=planes_ref.at[slot], send_sem=z_ss.at[slot],
            recv_sem=z_rs.at[slot], device_id={"zslab": slab + step}, device_id_type=MESH,
        )

    odd = slab % 2
    near_copy = pltpu.make_async_remote_copy(
        src_ref=meas_ref, dst_ref=near_ref, send_sem=h_ss.at[0], recv_sem=h_rs.at[0],
        device_id={"zslab": slab + 1 - 2 * odd}, device_id_type=MESH,
    )
    far_step = 2 * odd - 1
    far_valid = jnp.logical_and(slab + far_step >= 0, slab + far_step < slabs)
    far_copy = pltpu.make_async_remote_copy(
        src_ref=edge_ref, dst_ref=far_ref, send_sem=h_ss.at[1], recv_sem=h_rs.at[1],
        device_id={"zslab": slab + far_step}, device_id_type=MESH,
    )

    loads = [
        pltpu.make_async_copy(source, target, load_sem.at[n])
        for n, (source, target) in enumerate([
            (slot_hbm, slot_ref), (off_hbm, off_ref), (frame_hbm, frame_ref), (basis_hbm, basis_ref),
            (meas_hbm, meas_ref), (cone_hbm, cone_ref), (w_hbm, w_ref),
        ])
    ]
    sent = []

    def send(copy, valid=None):
        if valid is None:
            copy.start()
        else:
            pl.when(valid)(copy.start)
        sent.append((copy, valid))

    def finish():
        for copy, valid in sent:
            if valid is None:
                copy.wait_send()
            else:
                pl.when(valid)(copy.wait_send)

    barrier = pltpu.get_barrier_semaphore()
    for step in sorted(range(1, slabs), key=lambda d: -min(d, slabs - d)):
        pl.semaphore_signal(
            barrier, inc=1, device_id={"zslab": lax.rem(slab + step, slabs)}, device_id_type=MESH
        )
    for step in a_steps:
        pl.semaphore_signal(barrier, inc=1, device_id={"angle": a_device(step)}, device_id_type=MESH)
    for step in b_steps:
        pl.semaphore_signal(barrier, inc=1, device_id={"angle": b_device(step)}, device_id_type=MESH)
    for load in loads:
        load.start()

    for load in loads[:4]:
        load.wait()
    slots = [slot_ref[p] for p in range(PROJ)]
    rows = iota((PROJ * TILES, ANG * TILES), 0)
    cols = iota((PROJ * TILES, ANG * TILES), 1)
    slot_rows = jnp.concatenate(
        [jnp.full((TILES, ANG * TILES), slots[p], i32) for p in range(PROJ)], axis=0
    )
    pick = jnp.logical_and((rows & (TILES - 1)) == (cols & (TILES - 1)), slot_rows == (cols >> 4))
    offs = off_ref[...].reshape(ANG * TILES, na * nb).astype(f32).astype(bf16)
    offs_p = mm(pick.astype(f32).astype(bf16), offs)
    offs_sent = []
    order = iota((na * nb, na * nb), 0)
    for o_alpha, o_beta in ((order // nb, order % nb), (order % na, order // na)):
        image_row = (o_beta // nx) * (nz * nx) + o_alpha * nx + o_beta % nx
        permute = (image_row == iota((na * nb, na * nb), 1)).astype(f32).astype(bf16)
        offs_sent.append(mm(permute, offs_p.astype(bf16), NT))

    lane_p = iota((32, TILE), 1) >> 4
    frames = jnp.zeros((32, TILE), i32)
    for p in range(PROJ):
        frames = jnp.where(lane_p == p, frame_ref[p], frames)
    hot = (frames == iota((32, TILE), 0)).astype(f32)
    phi = lax.dot_general(
        basis_ref[...], hot, NN, precision=lax.Precision.HIGHEST, preferred_element_type=f32
    )
    rows_p = iota((PROJ, 32), 0)
    frames = jnp.zeros((PROJ, 32), i32)
    for p in range(PROJ):
        frames = jnp.where(rows_p == p, frame_ref[p], frames)
    hot = (frames == iota((PROJ, 32), 1)).astype(f32)
    phi_rows = lax.dot_general(
        hot, jnp.concatenate([basis_ref[...]] * TILES, axis=0), NT,
        precision=lax.Precision.HIGHEST, preferred_element_type=f32,
    )
    for v in range(VIEWS):
        (ng, me, *_), (ns, *_) = groups[v], groups[1 - v]
        for g in range(ng):
            meta_send[v, g, 0:ns, :] = offs_sent[v][g * ns:(g + 1) * ns]
            meta_send[v, g, 8:16, :] = phi
            meta_send[v, g, 16:24, :] = phi_rows
        meta_recv[v, me] = meta_send[v, me]

    for step in SLAB_OFFS:
        @pl.when(jnp.logical_not(z_valid(step)))
        def _():
            planes_ref[z_index(step)] = jnp.zeros((TILE, TILE), bf16)

    @pl.when(jnp.logical_not(far_valid))
    def _():
        far_ref[...] = jnp.zeros((TILE, TILE), bf16)

    for load in loads[4:]:
        load.wait()
    edge_ref[...] = meas_ref[...].astype(bf16)
    pl.semaphore_wait(barrier, len(a_steps) + len(b_steps) + slabs - 1)

    send(far_copy, far_valid)
    send(near_copy)
    for v in range(VIEWS):
        _, me, steps, at, _, _ = groups[v]
        for n, step in enumerate(steps):
            send(copy(0, v, 0, n, meta_send.at[v, at(step)], meta_recv.at[v, me]))

    def cone(kind, step, p):
        at = jnp.clip(slab + step, 0, slabs - 1)
        return cone_ref[kind, at, p]

    def cone_masked(kind, step, p):
        return jnp.where(z_valid(step), cone(kind, step, p), 0.0)

    def part(value, p):
        return value[p * TILES:(p + 1) * TILES]

    def back_of(below, here, above):
        return jnp.concatenate([
            cone_masked(0, 1, p) * part(above, p) + cone(1, 0, p) * part(here, p)
            + cone_masked(2, -1, p) * part(below, p)
            for p in range(PROJ)
        ], axis=0)

    def shift_up(value):
        return jnp.concatenate([value[1:], value[:1]], axis=0)

    def shift_down(value):
        return jnp.concatenate([value[-1:], value[:-1]], axis=0)

    weights = w_ref[...].reshape(ANG * TILE, 2 * TILE)
    slot_lane = jnp.concatenate(
        [jnp.full((8, TILES), slots[p], i32) for p in range(PROJ)], axis=1
    )

    def send_responses(phase, r_ref, back):
        high, low = split(jnp.concatenate([back, shift_up(back)], axis=1))
        owner = jnp.broadcast_to(slot_lane[:1], (UC, TILE))
        for v in range(VIEWS):
            ng, me, *_ = groups[v]
            some = jnp.concatenate([w_ref[a, v * UC:(v + 1) * UC, :] for a in range(ANG)], axis=0)
            every = mm(some, high, NT) + mm(some, low, NT)
            own = jnp.zeros((UC, TILE), f32)
            for a in range(ANG):
                own = jnp.where(owner == a, every[a * UC:(a + 1) * UC], own)
            r_ref[v, me] = own.astype(bf16)
            for n in range(ng - 1):
                send(copy(0, v, phase, n, r_ref.at[v, me], r_ref.at[v, me]))

    near_copy.wait_recv()
    pl.when(far_valid)(far_copy.wait_recv)
    measured = meas_ref[...]
    beside, beyond = near_ref[...], far_ref[...].astype(f32)
    below = jnp.where(odd == 1, beside, beyond)
    above = jnp.where(odd == 1, beyond, beside)
    send_responses(1, r1_ref, back_of(below, measured, above))

    e_row, e_col = iota((TILE, TILE), 0), iota((TILE, TILE), 1)
    same = (e_row >> 4) == (e_col >> 4)
    tile_row = iota((TILES, TILE), 0).astype(f32)
    tile_lane = (iota((BASIS, TILE), 1) & (TILES - 1)).astype(f32)
    def near_of(v):
        (ng, *_), (ns, *_) = groups[v], groups[1 - v]
        near = jnp.concatenate([meta_recv[v, g, 0:ns, :] for g in range(ng)], axis=0).astype(bf16)
        return ng, ns, near

    for v in (1, 0):
        wait_all(0, v, 0, lambda n, at: meta_recv.at[v, at])
        ng, ns, near = near_of(v)
        for p in range(PROJ):
            expand = jnp.logical_and(e_row >> 4 == p, (e_row & (TILES - 1)) == (e_col >> 3))
            xt_ref[v, p] = mm(near, expand.astype(f32).astype(bf16))

        def build_transposed(b, carry):
            at = pl.ds(pl.multiple_of(b * TILE, TILE), TILE)
            for g in range(ng):
                for p in range(PROJ):
                    line = xt_ref[v, p, pl.ds(g * ns + b, 1), :]
                    hit = jnp.broadcast_to(line, (TILES, TILE)) == tile_row
                    factor = jnp.broadcast_to(meta_recv[v, g, 16 + p:17 + p, :], (TILES, TILE))
                    mt_refs[v][g * TILE + p * TILES:g * TILE + (p + 1) * TILES, at] = jnp.where(
                        hit, factor, 0.0
                    ).astype(bf16)
            return carry

        lax.fori_loop(0, ns, build_transposed, 0)

    def build_plain():
        for v in (0, 1):
            ng, ns, near = near_of(v)
            for i in range(TILES):
                expand = jnp.logical_and(same, (e_row & (TILES - 1)) == i).astype(f32).astype(bf16)
                x_ref[v, i] = mm(near, expand)
            factors = [meta_recv[v, g, 8:16, :] for g in range(ng)]

            def build(b, carry):
                for pair in range(TILES // 2):
                    for g in range(ng):
                        lines = []
                        for i in (2 * pair, 2 * pair + 1):
                            line = x_ref[v, i, pl.ds(g * ns + b, 1), :]
                            hit = jnp.broadcast_to(line, (BASIS, TILE)) == tile_lane
                            lines.append(jnp.where(hit, factors[g], 0.0))
                        at = pl.ds(pl.multiple_of(b * TILE + pair * 16, 16), 16)
                        m_refs[v][at, g * TILE:(g + 1) * TILE] = jnp.concatenate(
                            lines, axis=0
                        ).astype(bf16)
                return carry

            lax.fori_loop(0, ns, build, 0)

    def wide(ref, c, count):
        return jnp.concatenate([ref[c, j] for j in range(count)], axis=1)

    def scatter_gradient(phase, g_phase, r_ref, p_send, p_recv, use, meanwhile=lambda: None):
        gathered = {}

        def rows_of(v, pair):
            some = jnp.concatenate(
                [mt_refs[v][:, pl.ds(pl.multiple_of(b * TILE, TILE), TILE)] for b in pair], axis=1
            )
            value = mm(gathered[v], some)
            return value[:, :TILE], value[:, TILE:]

        own = {}
        for v in (1, 0):
            (ng, *_), (_, _, steps, at_of, _, _) = groups[v], groups[1 - v]
            wait_all(0, v, g_phase, lambda n, at: r_ref.at[v, at])
            gathered[v] = wide(r_ref, v, ng)
            places = [at_of(step) for step in steps] + [groups[1 - v][1]]
            for n in range(0, len(places), 2):
                for m, value in zip((n, n + 1), rows_of(v, places[n:n + 2])):
                    if m == len(steps):
                        own[v] = value
                        continue
                    p_send[v, m] = value.astype(bf16)
                    send(copy(1, v, phase, m, p_send.at[v, m], p_recv.at[v, m]))
        meanwhile()
        for v in (1, 0):
            wait_all(1, v, phase, lambda n, at: p_recv.at[v, n])
            total = own[v]
            for n in range(groups[1 - v][0] - 1):
                total = total + p_recv[v, n].astype(f32)
            use(v, total)

    firsts = {}

    def use_first(v, total):
        ns, me, *_ = groups[1 - v]
        first = (STEP * total).astype(bf16)
        firsts[v] = first.astype(f32)
        first_ref[v, me] = first
        for n in range(ns - 1):
            send(copy(1, v, 1, n, first_ref.at[v, me], first_ref.at[v, me]))

    scatter_gradient(0, 1, r1_ref, p1_send, p1_recv, use_first, build_plain)
    fields = []

    def sums_of(v, pair):
        some = jnp.concatenate(
            [m_refs[v][:, pl.ds(pl.multiple_of(g * TILE, TILE), TILE)] for g in pair], axis=1
        )
        value = mm(fields[v], some)
        return value[:, :TILE], value[:, TILE:]

    sums = {}
    for v in (0, 1):
        (_, _, steps, at_of, _, _), (ns, *_) = groups[v], groups[1 - v]
        wait_all(1, v, 1, lambda n, at: first_ref.at[v, at])
        fields.append(wide(first_ref, v, ns))
        places = [at_of(step) for step in steps] + [groups[v][1]]
        for n in range(0, len(places), 2):
            for m, value in zip((n, n + 1), sums_of(v, places[n:n + 2])):
                if m == len(steps):
                    sums[v] = value
                    continue
                s_send[v, m] = value.astype(bf16)
                send(copy(0, v, 2, m, s_send.at[v, m], s_recv.at[v, m]))
    for v in (0, 1):
        wait_all(0, v, 2, lambda n, at: s_recv.at[v, n])
        for n in range(groups[v][0] - 1):
            sums[v] = sums[v] + s_recv[v, n].astype(f32)
    blank = jnp.zeros((TILES, TILE), bf16)
    halves = split(jnp.concatenate([sums[0], sums[1]], axis=0).T)
    masked = jnp.concatenate([
        jnp.concatenate(
            [jnp.where(slots[p] == a, part(half, p), blank) for half in halves for a in range(ANG)],
            axis=1,
        )
        for p in range(PROJ)
    ], axis=0)
    landed = mm(masked, jnp.concatenate([weights, weights], axis=0))
    plane = landed[:, :TILE] + shift_down(landed[:, TILE:])
    plane_ref[...] = plane.astype(bf16)
    for step in SLAB_OFFS:
        send(z_copy(step), z_valid(step))
    for step in SLAB_OFFS:
        pl.when(z_valid(step))(z_arrival(step).wait_recv)
    planes = {step: planes_ref[z_index(step)].astype(f32) for step in SLAB_OFFS}
    planes[0] = plane
    seen = {-1: below, 0: measured, 1: above}

    def misfit_at(v):
        return jnp.concatenate([
            cone(0, v, p) * part(planes[v - 1], p) + cone(1, v, p) * part(planes[v], p)
            + cone(2, v, p) * part(planes[v + 1], p) - part(seen[v], p)
            for p in range(PROJ)
        ], axis=0)

    misfit = misfit_at(0)
    misfit_ref[...] = misfit

    send_responses(3, r2_ref, back_of(misfit_at(-1), misfit, misfit_at(1)))
    updates = {}
    scatter_gradient(2, 3, r2_ref, p2_send, p2_recv, updates.__setitem__)
    rows_now = jnp.concatenate(
        [firsts[v] - STEP * updates[v] for v in range(VIEWS)], axis=0
    ).T.astype(bf16)
    coef_ref[...] = jnp.concatenate(
        [rows_now[i * BASIS:(i + 1) * BASIS] for i in range(TILES)], axis=1
    )

    finish()


def local(grid, slabs, measured, basis_time, frame_index, angle_slot, proj_weights, tile_offsets, cone_weights):
    ny, nz, nx = grid
    na, nb = nz, ny * nx
    most = max(na, nb)
    block, blocks = (TILE, TILE), (VIEWS, most, UC, TILE)
    vmem = pl.BlockSpec(memory_space=pltpu.VMEM)
    hbm = pl.BlockSpec(memory_space=pltpu.HBM)
    coefficients, misfit = pl.pallas_call(
        functools.partial(kernel, grid, slabs),
        out_shape=(
            pltpu.VMEM((BASIS, TILES * TILE), bf16),
            pltpu.VMEM(block, f32),
        ),
        in_specs=[hbm] * 7,
        out_specs=(vmem, vmem),
        scratch_shapes=[
            pltpu.VMEM(block, f32),
            pltpu.VMEM((BASIS, 32), f32),
            pltpu.SMEM((PROJ,), i32),
            pltpu.SMEM((PROJ,), i32),
            pltpu.VMEM((ANG, TILE, 2 * TILE), bf16),
            pltpu.VMEM((ANG, TILES, na * nb), i32),
            pltpu.SMEM((3, slabs, PROJ), f32),
            pltpu.SemaphoreType.DMA((7,)),
            pltpu.VMEM((VIEWS, most, 24, TILE), f32),
            pltpu.VMEM((VIEWS, most, 24, TILE), f32),
            pltpu.VMEM((VIEWS, TILES, na * nb, TILE), f32),
            pltpu.VMEM((VIEWS, PROJ, na * nb, TILE), f32),
            pltpu.VMEM((nb * TILE, na * TILE), bf16),
            pltpu.VMEM((na * TILE, nb * TILE), bf16),
            pltpu.VMEM((na * TILE, nb * TILE), bf16),
            pltpu.VMEM((nb * TILE, na * TILE), bf16),
            pltpu.VMEM(block, f32),
            pltpu.VMEM(block, bf16),
            pltpu.VMEM(block, bf16),
            pltpu.VMEM(block, bf16),
            pltpu.VMEM((4,) + block, bf16),
            pltpu.VMEM(blocks, bf16),
            pltpu.VMEM(blocks, bf16),
            pltpu.VMEM(blocks, bf16),
            pltpu.VMEM(blocks, bf16),
            pltpu.VMEM(blocks, bf16),
            pltpu.VMEM(blocks, bf16),
            pltpu.VMEM(blocks, bf16),
            pltpu.VMEM(blocks, bf16),
            pltpu.VMEM(blocks, bf16),
            pltpu.SemaphoreType.DMA((VIEWS, 4, most - 1)),
            pltpu.SemaphoreType.DMA((VIEWS, 4, most - 1)),
            pltpu.SemaphoreType.DMA((VIEWS, 3, most - 1)),
            pltpu.SemaphoreType.DMA((VIEWS, 3, most - 1)),
            pltpu.SemaphoreType.DMA((4,)),
            pltpu.SemaphoreType.DMA((4,)),
            pltpu.SemaphoreType.DMA((2,)),
            pltpu.SemaphoreType.DMA((2,)),
        ],
        compiler_params=pltpu.CompilerParams(
            collective_id=0, has_side_effects=True, vmem_limit_bytes=62 * 1000 * 1000
        ),
        name="two_gradients",
    )(
        measured.reshape(block),
        basis_time.T,
        frame_index,
        angle_slot,
        proj_weights,
        tile_offsets.transpose(0, 2, 1),
        cone_weights.transpose(0, 2, 1),
    )
    return (
        coefficients.reshape(1, BASIS, 1, TILES * TILE),
        misfit.reshape(PROJ, 1, TILES * TILE),
    )


def solution(mesh):
    placed = (
        P("angle", "zslab", None),
        P(),
        P("angle"),
        P("angle"),
        P("angle", None, None),
        P("angle", None, None),
        P(None, "angle", None),
    )
    grid = GRIDS[mesh.shape["angle"]]
    return jax.shard_map(
        functools.partial(local, grid, mesh.shape["zslab"]),
        mesh=mesh,
        in_specs=placed,
        out_specs=(P("angle", None, "zslab", None), P("angle", "zslab", None)),
        check_vma=False,
    )
```
